128 devices in a mesh: blk: 32 (over y_lo, x, z), dp: 4 (over y_hi, core).
Axes of the slice: x: 4, y: 4 (y_hi: 2, y_lo: 2; y = y_hi * 2 + y_lo), z: 4, core: 2. Of those that a mesh axis runs over, the one named last changes fastest.
Arguments:
- embeddings: bfloat16 [20480, 4096], P(('dp', 'blk')), parts along dimension 0, may hold values from -1 to 1
- partner: int32 [20480], P(('dp', 'blk')), parts along dimension 0, may hold values from 0 to 5119, as said below
- logit_scale: float32 [1], replicated, may hold values from 10 to 320
Outputs:
- grad: bfloat16 [20480, 4096], P(('dp', 'blk')), parts along dimension 0
- loss: float32 [4], P('dp'), parts along dimension 0
The draws below stay inside these ranges and needn't reach their ends.
There are 4 independent parts, one for each index of `dp`. The reference program is written for one: setup_inputs(seed, part) draws one part's arguments, and reference() takes and returns one part's arrays. A program takes and returns all parts, laid end to end along the dimension named above; an argument that names none is the same for every part. Nothing has to cross between parts.
Inputs may be any that keep to these rules, and one draw needn't show every extreme that they name: partner pairs the rows: partner[partner[i]] = i and partner[i] != i.
All inputs are finite; a program needn't handle non-finite values.
Results may differ from the reference program's by a relative error of at most 0.0019.
The reference program's roundings to bfloat16 on the way (of `unit` and `weights`) count: a program that leaves them out, or rounds other values in their place, can miss the bound.
Values may be sent and summed in bfloat16 or wider, within the bound.
No kernel may reach another device: no remote copies, remote signals or barrier semaphores. Data moves between devices by JAX's collectives and lax.ppermute only.
A program may use at most 128 MiB of HBM per device.

```python
import math
import jax
import jax.numpy as jnp
from jax import lax

D = 4096
TOKENS = 5120


def draw_embeddings(key, part):
    key = jax.random.fold_in(key, 1)
    key_base, key_rows, key_cols = jax.random.split(key, 3)
    rowscale = jnp.exp(jax.random.uniform(key_rows, (TOKENS, 1), jnp.float32, math.log(0.5), math.log(5.0)))
    colscale = jnp.exp(jax.random.uniform(key_cols, (1, D), jnp.float32, math.log(0.3), math.log(3.0)))
    base = jnp.clip(jax.random.normal(key_base, (TOKENS, D), jnp.float32), -4.0, 4.0)
    values = base * rowscale * colscale / math.sqrt(D)
    return jnp.clip(values, -1.0, 1.0).astype(jnp.bfloat16)


def draw_partner(key, part):
    key = jax.random.fold_in(key, 2)
    order = jax.random.permutation(key, TOKENS).astype(jnp.int32)
    flipped = jnp.bitwise_xor(jnp.arange(TOKENS, dtype=jnp.int32), 1)
    mates = order[flipped]
    return jnp.zeros((TOKENS,), jnp.int32).at[order].set(mates)


def draw_logit_scale(key, part):
    key = jax.random.fold_in(key, 3)
    return jax.random.uniform(key, (1,), jnp.float32, 10.0, 30.0)


def setup_inputs(seed: int = 0, part: int = 0) -> dict:
    keys = jax.random.split(jax.random.key(seed), 4)
    own_keys = jax.random.split(jax.random.fold_in(keys[3], part), 4)
    embeddings = draw_embeddings(jax.random.fold_in(jax.random.fold_in(keys[3], part), 71), part)
    partner = draw_partner(jax.random.fold_in(jax.random.fold_in(keys[3], part), 71), part)
    logit_scale = draw_logit_scale(jax.random.fold_in(keys[3], 71), part)
    return {"embeddings": embeddings, "partner": partner, "logit_scale": logit_scale}


def reference(embeddings, partner, logit_scale):
    wide = embeddings.astype(jnp.float32)
    factor = lax.rsqrt(lax.optimization_barrier(jnp.sum(wide * wide, axis=1, keepdims=True)) + 1e-06)
    unit = (wide * factor).astype(jnp.bfloat16)
    multiplier = logit_scale[0]
    slab = multiplier * lax.dot_general(unit, unit, (((1,), (1,)), ((), ())), preferred_element_type=jnp.float32)
    total = embeddings.shape[0]
    row_ids = lax.broadcasted_iota(jnp.int32, (total, 1), 0)
    col_ids = lax.broadcasted_iota(jnp.int32, (1, total), 1)
    diagonal = row_ids == col_ids
    masked = jnp.where(diagonal, jnp.float32(-1e+30), slab)
    highest = lax.optimization_barrier(jnp.max(masked, axis=1))
    lse = highest + jnp.log(lax.optimization_barrier(jnp.sum(jnp.exp(masked - highest[:, None]), axis=1)))
    onehot = col_ids == partner[:, None]
    positive = lax.optimization_barrier(jnp.sum(jnp.where(onehot, slab, jnp.float32(0.0)), axis=1))
    loss = (jnp.sum(lse - positive) / total).reshape(1)
    own = jnp.exp(masked - lse[:, None])
    other = jnp.exp(masked - lse[None, :])
    weights = (own + other - 2.0 * onehot.astype(jnp.float32)).astype(jnp.bfloat16)
    grad_unit = multiplier * jnp.dot(weights, unit, preferred_element_type=jnp.float32)
    inner = lax.optimization_barrier(jnp.sum(wide * grad_unit, axis=1, keepdims=True))
    grad = (factor * grad_unit - factor * factor * factor * inner * wide).astype(jnp.bfloat16)
    return (grad, loss)
```

```python
import jax
import jax.numpy as jnp
from jax import lax
from jax.sharding import Mesh, PartitionSpec as P

X, Z = 4, 4


def ring(n, step):
    return [(i, (i + step) % n) for i in range(n)]


SWAP = [(0, 0), (1, 2), (2, 1), (3, 3)]
SWAP_OTHER = [(1, 0), (3, 1), (0, 2), (2, 3)]


def swap(v):
    return lax.ppermute(v, ("yl", "c"), SWAP)


def other_core(v):
    return lax.ppermute(v, "c", ring(2, 1))


def gather_ring(u, axis):
    half = u.shape[0] // 2
    down = lax.ppermute(u, axis, ring(4, 1))
    up = lax.ppermute(u, axis, ring(4, -1))
    first = lax.ppermute(down[:half], axis, ring(4, 1))
    second = lax.ppermute(up[half:], axis, ring(4, -1))
    return [u, up, jnp.concatenate([first, second], 0), down]


def gather_small(v, axis):
    return [v] + [lax.ppermute(v, axis, ring(4, -k)) for k in (1, 2, 3)]


def scatter_ring(parts, axis):
    half = parts[0].shape[0] // 2
    t1 = lax.ppermute(parts[2][:half], axis, ring(4, 1))
    t2 = lax.ppermute(parts[2][half:], axis, ring(4, -1))
    d1 = lax.ppermute(parts[1][half:], axis, ring(4, 1))
    d3 = lax.ppermute(parts[3][:half], axis, ring(4, -1))
    s1 = lax.ppermute(t1 + parts[1][:half], axis, ring(4, 1))
    s3 = lax.ppermute(t2 + parts[3][half:], axis, ring(4, -1))
    return jnp.concatenate([parts[0][:half] + s1 + d3, parts[0][half:] + s3 + d1], 0)


def local(embeddings, partner, logit_scale):
    rows, width = embeddings.shape
    half = width // 2
    total = rows * 2 * X * Z
    multiplier = logit_scale[0]
    c, x, z = lax.axis_index("c"), lax.axis_index("x"), lax.axis_index("z")

    emb = swap(embeddings)
    mate = swap(partner.reshape(1, rows))
    wide = emb.astype(jnp.float32)
    factor = lax.rsqrt(jnp.sum(wide * wide, axis=1, keepdims=True) + 1e-06)
    unit = (wide * factor).astype(jnp.bfloat16)

    a_own = gather_ring(unit, "z")
    b_own = gather_ring(unit, "x")
    b_other = [other_core(v) for v in b_own]
    a_other = [other_core(v[:, half:]) for v in a_own]
    mates = jnp.concatenate(gather_small(mate, "z"), 1).reshape(-1, 1)

    a_rows = jnp.concatenate(a_own, 0)
    b_rows = jnp.concatenate(b_own + b_other, 0)
    scores = multiplier * lax.dot_general(
        a_rows, b_rows, (((1,), (1,)), ((), ())), preferred_element_type=jnp.float32
    )
    within = jnp.arange(rows, dtype=jnp.int32)
    row_ids = jnp.concatenate(
        [((c * X + x) * Z + (z + k) % Z) * rows + within for k in range(4)]
    ).reshape(-1, 1)
    col_ids = jnp.concatenate(
        [((cc * X + (x + k) % X) * Z + z) * rows + within for cc in (c, 1 - c) for k in range(4)]
    ).reshape(1, -1)
    onehot = col_ids == mates
    masked = jnp.where(row_ids == col_ids, jnp.float32(-1e30), scores)
    top = jnp.max(masked, axis=1)
    low = jnp.sum(jnp.exp(masked - top[:, None]), axis=1)
    pos = jnp.sum(jnp.where(onehot, scores, jnp.float32(0.0)), axis=1)
    stats = jnp.stack(gather_small(jnp.stack([top, low, pos]), "z"))
    stats = stats.reshape(4, 3, 4, rows)
    stats = jnp.stack([jnp.roll(stats[s], s, axis=1) for s in range(4)]).reshape(4, 3, -1)
    highest = jnp.max(stats[:, 0], axis=0)
    lse = highest + jnp.log(jnp.sum(stats[:, 1] * jnp.exp(stats[:, 0] - highest), axis=0))
    positive = jnp.sum(stats[:, 2], axis=0)

    own = lse[:rows].reshape(1, rows)
    lse_own = gather_small(own, "x")
    lse_cols = jnp.concatenate(lse_own + [other_core(v) for v in lse_own], 1)
    weights = (
        jnp.exp(masked - lse[:, None])
        + jnp.exp(masked - lse_cols)
        - 2.0 * onehot.astype(jnp.float32)
    ).astype(jnp.bfloat16)

    near, far = weights[:, : 4 * rows], weights[:, 4 * rows :]
    far = other_core(far)
    g_z = jnp.dot(weights, b_rows[:, :half], preferred_element_type=jnp.float32)
    a_half = jnp.concatenate([v[:, half:] for v in a_own] + a_other, 0)
    g_x = lax.dot_general(
        jnp.concatenate([near, far], 0), a_half, (((0,), (0,)), ((), ())),
        preferred_element_type=jnp.float32,
    )
    cut = lambda g: [g[k * rows : (k + 1) * rows] for k in range(4)]
    sum_z = scatter_ring(cut(g_z), "z")
    sum_x = scatter_ring(cut(g_x), "x")
    grad_unit = multiplier * jnp.concatenate([sum_z, sum_x], 1)
    inner = jnp.sum(wide * grad_unit, axis=1, keepdims=True)
    grad = (factor * grad_unit - factor * factor * factor * inner * wide).astype(jnp.bfloat16)

    part = jnp.sum(lse - positive).reshape(1, 1)
    part = sum(gather_small(part, "x"))
    both = swap(part) + lax.ppermute(part, ("yl", "c"), SWAP_OTHER)
    return swap(grad), (both / total).reshape(1)


def solution(mesh):
    fine = Mesh(
        mesh.devices.reshape(2, X, Z, 2, 2), ("yl", "x", "z", "yh", "c")
    )
    rows = ("yh", "c", "yl", "x", "z")
    return jax.shard_map(
        local,
        mesh=fine,
        in_specs=(P(rows, None), P(rows), P()),
        out_specs=(P(rows, None), P(("yh", "c"))),
        check_vma=False,
    )
```

```python
import math

import jax
import jax.numpy as jnp
from jax import lax
from jax.experimental import pallas as pl
from jax.experimental.pallas import tpu as pltpu
from jax.sharding import Mesh, PartitionSpec as P

X, Z = 4, 4
ORDER = (0, 1, 3, 2)
LANES = 128
LEVELS = 32000.0
STEPS = 64 / math.log(2.0)
NN = (((1,), (0,)), ((), ()))
NT = (((1,), (1,)), ((), ()))
TN = (((0,), (0,)), ((), ()))
F32, BF16, I16 = jnp.float32, jnp.bfloat16, jnp.int16


def ring(n, step):
    return [(i, (i + step) % n) for i in range(n)]


SWAP = [(0, 0), (1, 2), (2, 1), (3, 3)]
SWAP_OTHER = [(1, 0), (3, 1), (0, 2), (2, 3)]


def swap(v):
    return lax.ppermute(v, ("yl", "c"), SWAP)


def other_core(v):
    return lax.ppermute(v, "c", ring(2, 1))


def up(v, axis):
    return lax.ppermute(v, axis, ring(4, 1))


def down(v, axis):
    return lax.ppermute(v, axis, ring(4, -1))


def after(v, *others):
    return lax.optimization_barrier((v, *others))[0]


def gather_small(v, axis):
    return [v] + [lax.ppermute(v, axis, ring(4, -k)) for k in ORDER[1:]]


def dot(a, b, dims):
    return lax.dot_general(a, b, dims, preferred_element_type=F32)


def call(kernel, name, args, outs, scratch=(), flops=0):
    vmem = pl.BlockSpec(memory_space=pltpu.VMEM)
    smem = pl.BlockSpec(memory_space=pltpu.SMEM)
    size = sum(a.size * a.dtype.itemsize for a in list(args) + list(outs))
    return pl.pallas_call(
        kernel,
        name=name,
        out_shape=tuple(jax.ShapeDtypeStruct(o.shape, o.dtype) for o in outs),
        in_specs=[smem if a.shape == (1,) else vmem for a in args],
        out_specs=tuple(vmem for _ in outs),
        scratch_shapes=list(scratch),
        cost_estimate=pl.CostEstimate(flops=flops, bytes_accessed=size, transcendentals=0),
        compiler_params=pltpu.CompilerParams(vmem_limit_bytes=16 << 20),
    )(*args)


def shape(*dims, dtype=F32):
    return jax.ShapeDtypeStruct(dims, dtype)


def split_kernel(xu, xd, zu, zd, xa, xb, za, zb):
    cut = xa.shape[0]
    xa[...] = xu[0:cut, :]
    za[...] = zu[0:cut, :]
    xb[...] = xd[cut:, :]
    zb[...] = zd[cut:, :]


def stack_kernel(u, xd, xu, zd, zu, be, ae):
    rows = u.shape[0]
    for dst, d, w in ((be, xd, xu), (ae, zd, zu)):
        dst[0:rows, :] = u[...]
        dst[rows : 2 * rows, :] = d[...]
        dst[2 * rows :, :] = w[...]


def early_kernel(ae, b, s):
    s[...] = dot(ae[...], b[...], NT)


def column(row, n):
    return jnp.transpose(jnp.broadcast_to(row, (LANES, n)))[:, :1]


def tail_kernel(mult, ae, za, zb, bo, xa, xb, bs, ya, yb, s1, s2, mate, s, rstat, cstat, at, bt):
    n, side = bo.shape[0], s.shape[1] // 2
    cut, rows = za.shape[0], 2 * za.shape[0]
    for i, v in enumerate((za, zb)):
        at[i * cut : (i + 1) * cut, :] = v[...]
    for i, v in enumerate((xa, xb, ya, yb)):
        bt[i * cut : (i + 1) * cut, :] = v[...]
    s[0:n, 0:n] = s1[...]
    s[0:n, side : side + n] = s2[...]
    s[n:, 0:n] = dot(at[...], bo[...], NT)
    s[n:, side : side + n] = dot(at[...], bs[...], NT)
    e = dot(ae[...], bt[...], NT)
    s[0:n, n:side] = e[:, :rows]
    s[0:n, side + n :] = e[:, rows:]
    e = dot(at[...], bt[...], NT)
    s[n:, n:side] = e[:, :rows]
    s[n:, side + n :] = e[:, rows:]
    multiplier = mult[0]
    tall, wide = s.shape
    rstat[...] = jnp.zeros(rstat.shape, F32)
    rstat[2:3, 0:rows] = mate[...]

    def first(i, top):
        r = pl.ds(pl.multiple_of(i * LANES, LANES), LANES)
        v = s[r, :] * multiplier
        row_ids = i * LANES + lax.broadcasted_iota(jnp.int32, (LANES, wide), 0)
        col_ids = lax.broadcasted_iota(jnp.int32, (LANES, wide), 1)
        v = jnp.where((row_ids == col_ids) & (row_ids < rows), F32(-1e30), v)
        s[r, :] = v
        m = jnp.max(v, axis=1, keepdims=True)
        l = jnp.sum(jnp.exp(v - m), axis=1, keepdims=True)
        rstat[0:1, r] = jnp.transpose(jnp.broadcast_to(m, (LANES, LANES)))[0:1, :]
        rstat[1:2, r] = jnp.transpose(jnp.broadcast_to(l, (LANES, LANES)))[0:1, :]
        return jnp.maximum(top, jnp.max(v, axis=0, keepdims=True))

    top = lax.fori_loop(0, tall // LANES, first, jnp.full((1, wide), -1e30, F32))

    def second(i, low):
        r = pl.ds(pl.multiple_of(i * LANES, LANES), LANES)
        return low + jnp.sum(jnp.exp(s[r, :] - top), axis=0, keepdims=True)

    low = lax.fori_loop(0, tall // LANES, second, jnp.zeros((1, wide), F32))
    cstat[...] = jnp.zeros(cstat.shape, F32)
    cstat[0:1, :] = top
    cstat[1:2, :] = low


def merge_kernel(mine, other, s, r0, r1, r2, r3, cols, out, known):
    side = mine.shape[1] // 2
    tall, wide = s.shape
    rows = tall // 4
    theirs = jnp.concatenate([other[:, side:], other[:, :side]], 1)
    m1, m2 = mine[0:1, :], theirs[0:1, :]
    m = jnp.maximum(m1, m2)
    out[0:1, :] = m
    out[1:2, :] = mine[1:2, :] * jnp.exp(m1 - m) + theirs[1:2, :] * jnp.exp(m2 - m)
    lse_r = combine((r0, r1, r2, r3), rows)
    known[...] = jnp.zeros(known.shape, F32)
    known[0:1, :] = lse_r
    known[1:2, :] = jnp.concatenate([r[2:3, 0:rows] for r in (r0, r1, r2, r3)], 1)
    ids = cols[...]

    def step(i, pos):
        r = pl.ds(pl.multiple_of(i * LANES, LANES), LANES)
        hit = ids == column(known[1:2, r], LANES)
        return pos + jnp.sum(jnp.where(hit, s[r, :], F32(0.0)), axis=0, keepdims=True)

    pos = lax.fori_loop(0, tall // LANES, step, jnp.zeros((1, wide), F32))
    share = jnp.sum(lse_r[:, 0:rows]) - jnp.sum(pos)
    out[2:3, :] = jnp.full((1, wide), share, F32)
    out[3:, :] = jnp.zeros((out.shape[0] - 3, wide), F32)


def combine(messages, rows):
    groups = messages[0].shape[1] // (4 * rows)
    tops, lows = [], []
    for step, message in zip(ORDER, messages):
        at = [(g * 4 + ORDER.index((k - step) % 4)) * rows for g in range(groups) for k in ORDER]
        tops.append(jnp.concatenate([message[0:1, p : p + rows] for p in at], 1))
        lows.append(jnp.concatenate([message[1:2, p : p + rows] for p in at], 1))
    top = jnp.maximum(jnp.maximum(tops[0], tops[1]), jnp.maximum(tops[2], tops[3]))
    low = sum(l * jnp.exp(t - top) for t, l in zip(tops, lows))
    return top + jnp.log(low)


def weights_kernel(s, known, c0, c1, c2, c3, cols, near, far, part):
    tall, wide = s.shape
    side = wide // 2
    lse_c = combine((c0, c1, c2, c3), tall // 4)
    ids = cols[...]

    @pl.loop(0, tall // LANES)
    def _(i):
        r = pl.ds(pl.multiple_of(i * LANES, LANES), LANES)
        v = s[r, :]
        hit = ids == column(known[1:2, r], LANES)
        w = jnp.exp(v - column(known[0:1, r], LANES)) + jnp.exp(v - lse_c)
        w = (w - jnp.where(hit, F32(2.0), F32(0.0))).astype(BF16)
        near[r, :] = w[:, :side]
        far[r, :] = w[:, side:]

    part[...] = c0[2:3, 0:LANES] + c1[2:3, 0:LANES] + c2[2:3, 0:LANES] + c3[2:3, 0:LANES]


def pack(dst, at, g):
    n, w = g.shape
    m = jnp.maximum(jnp.max(jnp.abs(g), axis=1, keepdims=True), F32(1e-30))
    k = jnp.ceil(jnp.log(m) * STEPS)
    q = (g * (LEVELS * jnp.exp(k * (-1.0 / STEPS))) + F32(12582912.0)) - F32(12582912.0)
    dst[at : at + n, 0:w] = q.astype(jnp.int32).astype(I16)
    dst[at : at + n, w : w + LANES] = jnp.broadcast_to(k, (n, LANES)).astype(jnp.int32).astype(I16)


def unpack(src, at, n):
    w = src.shape[1] - LANES
    k = src[at : at + n, w : w + LANES].astype(jnp.int32).astype(F32)[:, :1]
    q = src[at : at + n, 0:w].astype(jnp.int32).astype(F32)
    return q * (jnp.exp(k * (1.0 / STEPS)) * (1.0 / LEVELS))


def hand_out(acc, fwd, bwd, keep1, keep3, own):
    rows = own.shape[0]
    cut = rows // 2
    pack(fwd, 0, acc[3 * rows : 3 * rows + cut, :])
    pack(fwd, cut, acc[rows + cut : 2 * rows, :])
    pack(bwd, 0, acc[3 * rows + cut : 4 * rows, :])
    pack(bwd, cut, acc[2 * rows : 2 * rows + cut, :])
    keep1[...] = acc[rows : rows + cut, :]
    keep3[...] = acc[2 * rows + cut : 3 * rows, :]
    own[...] = acc[0:rows, :]


def rows_z_kernel(bo, xa, xb, bs, ya, yb, out):
    n, cut, half = bo.shape[0], xa.shape[0], out.shape[1]
    at = 0
    for v in (bo, xa, xb, bs, ya, yb):
        out[at : at + v.shape[0], :] = v[:, :half]
        at += v.shape[0]


def rows_x_kernel(ae, za, zb, oe, oa, ob, out):
    half = out.shape[1]
    at = 0
    for v in (ae, za, zb, oe, oa, ob):
        out[at : at + v.shape[0], :] = v[:, v.shape[1] - half :]
        at += v.shape[0]


def z_kernel(near, far, b, fwd, bwd, keep1, keep3, own, acc):
    side = near.shape[1]
    acc[...] = dot(near[...], b[0:side, :], NN) + dot(far[...], b[side:, :], NN)
    hand_out(acc, fwd, bwd, keep1, keep3, own)


def x_kernel(near, far, a, fwd, bwd, keep1, keep3, own, acc):
    side = near.shape[0]
    acc[...] = dot(near[...], a[0:side, :], TN) + dot(far[...], a[side:, :], TN)
    hand_out(acc, fwd, bwd, keep1, keep3, own)


def forward_kernel(fwd, bwd, keep1, keep3, to_up, to_down):
    cut = keep1.shape[0]
    pack(to_up, 0, unpack(fwd, 0, cut) + keep1[...])
    pack(to_down, 0, unpack(bwd, 0, cut) + keep3[...])


def finish_kernel(mult, e, oz, fz, bz, uz, dz, ox, fx, bx, ux, dx, grad):
    cut, half = e.shape[0] // 2, oz.shape[1]
    for h in (0, 1):
        r = slice(h * cut, (h + 1) * cut)
        terms = []
        for own, f, b, u, d in ((oz, fz, bz, uz, dz), (ox, fx, bx, ux, dx)):
            step, straight = (u, b) if h == 0 else (d, f)
            terms.append(own[r, :] + unpack(step, 0, cut) + unpack(straight, cut, cut))
        g0, g1 = mult[0] * terms[0], mult[0] * terms[1]
        e0, e1 = e[r, :half].astype(F32), e[r, half:].astype(F32)
        square = jnp.sum(e0 * e0, axis=1, keepdims=True) + jnp.sum(e1 * e1, axis=1, keepdims=True)
        factor = lax.rsqrt(square + 1e-06)
        inner = jnp.sum(e0 * g0, axis=1, keepdims=True) + jnp.sum(e1 * g1, axis=1, keepdims=True)
        scale = factor * factor * factor * inner
        grad[r, :half] = (factor * g0 - scale * e0).astype(BF16)
        grad[r, half:] = (factor * g1 - scale * e1).astype(BF16)


def normalize(e):
    wide = e.astype(F32)
    return (wide * lax.rsqrt(jnp.sum(wide * wide, axis=1, keepdims=True) + 1e-06)).astype(BF16)


def local(embeddings, partner, logit_scale):
    rows, width = embeddings.shape
    half, cut = width // 2, rows // 2
    side, n = 4 * rows, 3 * rows
    total = rows * 2 * X * Z
    c, x, z = lax.axis_index("c"), lax.axis_index("x"), lax.axis_index("z")

    emb = swap(embeddings)
    u = normalize(emb)

    xu, xd, zu, zd = lax.optimization_barrier((up(u, "x"), down(u, "x"), up(u, "z"), down(u, "z")))
    piece = shape(cut, width, dtype=BF16)
    xa, xb, za, zb = call(split_kernel, "halves", (xu, xd, zu, zd), (piece,) * 4)
    xa, za, xb, zb = up(xa, "x"), up(za, "z"), down(xb, "x"), down(zb, "z")
    stack = shape(n, width, dtype=BF16)
    be, ae = call(stack_kernel, "stack", (u, xd, xu, zd, zu), (stack, stack))
    flops = 2 * n * n * width
    scores1, = call(early_kernel, "early", (ae, be), (shape(n, n),), flops=flops)
    be, scores1 = lax.optimization_barrier((be, scores1))
    bs = other_core(be)
    mate = swap(after(partner.reshape(1, rows), scores1)).astype(F32)
    xa, xb, za, zb = lax.optimization_barrier((xa, xb, za, zb))
    ya, yb = other_core(xa), other_core(xb)
    scores2, = call(early_kernel, "other", (ae, bs), (shape(n, n),), flops=flops)
    oe = other_core(after(ae, ya, yb))
    oa, ob = other_core(after(za, oe)), other_core(after(zb, oe))

    scores, rstat, cstat = call(
        tail_kernel, "tail", (logit_scale, ae, za, zb, be, xa, xb, bs, ya, yb, scores1, scores2, mate),
        (shape(side, 2 * side), shape(8, side), shape(8, 2 * side)),
        scratch=[pltpu.VMEM((rows, width), BF16), pltpu.VMEM((2 * rows, width), BF16)],
        flops=2 * 7 * rows * 2 * rows * width,
    )
    within = jnp.arange(rows, dtype=jnp.int32)
    cols = jnp.concatenate(
        [((cc * X + (x + k) % X) * Z + z) * rows + within for cc in (c, 1 - c) for k in ORDER]
    ).reshape(1, -1).astype(F32)
    cstat_other = other_core(cstat)
    rstats = gather_small(rstat, "z")
    merged, known = call(
        merge_kernel, "merge", (cstat, cstat_other, scores, *rstats, cols), (cstat, rstat)
    )
    cstats = gather_small(merged, "x")
    near, far, part = call(
        weights_kernel, "weights", (scores, known, *cstats, cols),
        (shape(side, side, dtype=BF16), shape(side, side, dtype=BF16), shape(1, LANES)),
    )
    far_other = other_core(far)

    stack = shape(2 * side, half, dtype=BF16)
    rows_z, = call(rows_z_kernel, "rows_z", (be, xa, xb, bs, ya, yb), (stack,))
    rows_x, = call(rows_x_kernel, "rows_x", (ae, za, zb, oe, oa, ob), (stack,))
    message = shape(rows, half + LANES, dtype=I16)
    kept = shape(cut, half)
    outs = (message, message, kept, kept, shape(rows, half))
    flops = 2 * side * 2 * side * half
    acc = [pltpu.VMEM((side, half), F32)]
    fz, bz, k1z, k3z, oz = call(
        z_kernel, "along_z", (near, far, rows_z), outs, scratch=acc, flops=flops
    )
    fz, bz = up(fz, "z"), down(bz, "z")
    fx, bx, k1x, k3x, ox = call(
        x_kernel, "along_x", (near, far_other, rows_x), outs, scratch=acc, flops=flops
    )
    fx, bx = up(fx, "x"), down(bx, "x")
    fz, bz, part = lax.optimization_barrier((fz, bz, sum(gather_small(part, "z"))))
    both = swap(part) + lax.ppermute(part, ("yl", "c"), SWAP_OTHER)
    short = shape(cut, half + LANES, dtype=I16)
    uz, dz = call(forward_kernel, "forward_z", (fz, bz, k1z, k3z), (short, short))
    uz, dz = up(uz, "z"), down(dz, "z")
    fx, bx, both = lax.optimization_barrier((fx, bx, both))
    ux, dx = call(forward_kernel, "forward_x", (fx, bx, k1x, k3x), (short, short))
    ux, dx = up(ux, "x"), down(dx, "x")
    grad, = call(
        finish_kernel, "finish",
        (logit_scale, emb, oz, fz, bz, uz, dz, ox, fx, bx, ux, dx),
        (shape(rows, width, dtype=BF16),),
    )
    return swap(grad), (both[0, :1] / total)


def solution(mesh):
    fine = Mesh(
        mesh.devices.reshape(2, X, Z, 2, 2), ("yl", "x", "z", "yh", "c")
    )
    rows = ("yh", "c", "yl", "x", "z")
    return jax.shard_map(
        local,
        mesh=fine,
        in_specs=(P(rows, None), P(rows), P()),
        out_specs=(P(rows, None), P(("yh", "c"))),
        check_vma=False,
    )
```

```python
import math

import jax
import jax.numpy as jnp
from jax import lax
from jax.experimental import pallas as pl
from jax.experimental.pallas import tpu as pltpu
from jax.sharding import Mesh, PartitionSpec as P

X, Z = 4, 4
ORDER = (0, 1, 3, 2)
LANES = 128
LEVELS = 32000.0
STEPS = 64 / math.log(2.0)
NN = (((1,), (0,)), ((), ()))
NT = (((1,), (1,)), ((), ()))
TN = (((0,), (0,)), ((), ()))
F32, BF16, I16 = jnp.float32, jnp.bfloat16, jnp.int16


def ring(n, step):
    return [(i, (i + step) % n) for i in range(n)]


SWAP = [(0, 0), (1, 2), (2, 1), (3, 3)]
SWAP_OTHER = [(1, 0), (3, 1), (0, 2), (2, 3)]


def swap(v):
    return lax.ppermute(v, ("yl", "c"), SWAP)


def other_core(v):
    return lax.ppermute(v, "c", ring(2, 1))


def up(v, axis):
    return lax.ppermute(v, axis, ring(4, 1))


def down(v, axis):
    return lax.ppermute(v, axis, ring(4, -1))


def after(v, *others):
    return lax.optimization_barrier((v, *others))[0]


def gather_small(v, axis):
    return [v] + [lax.ppermute(v, axis, ring(4, -k)) for k in ORDER[1:]]


def dot(a, b, dims):
    return lax.dot_general(a, b, dims, preferred_element_type=F32)


def call(kernel, name, args, outs, scratch=(), flops=0, mib=14):
    args = [
        pltpu.with_memory_space_constraint(a, pltpu.VMEM) if a.size * a.dtype.itemsize >= 1 << 19 else a
        for a in args
    ]
    vmem = pl.BlockSpec(memory_space=pltpu.VMEM)
    smem = pl.BlockSpec(memory_space=pltpu.SMEM)
    size = sum(a.size * a.dtype.itemsize for a in list(args) + list(outs))
    return pl.pallas_call(
        kernel,
        name=name,
        out_shape=tuple(jax.ShapeDtypeStruct(o.shape, o.dtype) for o in outs),
        in_specs=[smem if a.shape == (1,) else vmem for a in args],
        out_specs=tuple(vmem for _ in outs),
        scratch_shapes=list(scratch),
        cost_estimate=pl.CostEstimate(flops=flops, bytes_accessed=size, transcendentals=0),
        compiler_params=pltpu.CompilerParams(vmem_limit_bytes=mib << 20),
    )(*args)


def shape(*dims, dtype=F32):
    return jax.ShapeDtypeStruct(dims, dtype)


def halves_kernel(xu, xd, zu, zd, xa, xb, za, zb):
    cut = xa.shape[0]
    xa[...] = xu[0:cut, :]
    za[...] = zu[0:cut, :]
    xb[...] = xd[cut:, :]
    zb[...] = zd[cut:, :]


def stack_kernel(*refs):
    at = 0
    for v in refs[:-1]:
        refs[-1][at : at + v.shape[0], :] = v[...]
        at += v.shape[0]


def stack(name, *refs):
    out = shape(sum(r.shape[0] for r in refs), refs[0].shape[1], dtype=BF16)
    return call(stack_kernel, name, refs, (out,))[0]


def unit_kernel(e, digits, u, v):
    wide = e[...].astype(F32)
    unit = wide * lax.rsqrt(jnp.sum(wide * wide, axis=1, keepdims=True) + 1e-06)
    u[...] = unit.astype(BF16)
    v[:, : e.shape[1]] = unit.astype(BF16)
    v[:, e.shape[1] :] = digits[...]


def early_kernel(v, zd, zu, za, zb, b, a, last, mates, s):
    width, w = a.shape[1], last.shape[1]
    at = 0
    for r in (v, zd, zu, za, zb):
        n = r.shape[0]
        a[at : at + n, :] = r[:, :width]
        last[at : at + n, :] = r[:, width - w : width]
        two = r[:, width:].astype(F32)
        mates[at : at + n, :] = jnp.broadcast_to(two[:, 0:1] * F32(64.0) + two[:, 1:2], (n, LANES))
        at += n
    s[...] = dot(a[...], b[...], NT)


def column(row, n):
    return jnp.transpose(jnp.broadcast_to(row, (LANES, n)))[:, :1]


def tail_kernel(mult, a, b, early, mates, cols, s, rstat, cstat):
    side, rows = early.shape[0], early.shape[0] // 4
    s[:, 0:side] = early[...]
    s[:, side:] = dot(a[...], b[...], NT)
    multiplier = mult[0]
    tall, wide = s.shape
    rstat[...] = jnp.zeros(rstat.shape, F32)
    ids = cols[...]

    def first(i, carry):
        top, pos = carry
        r = pl.ds(pl.multiple_of(i * LANES, LANES), LANES)
        v = s[r, :] * multiplier
        pos += jnp.sum(jnp.where(ids == mates[r, 0:1], v, F32(0.0)), axis=0, keepdims=True)
        row_ids = i * LANES + lax.broadcasted_iota(jnp.int32, (LANES, wide), 0)
        col_ids = lax.broadcasted_iota(jnp.int32, (LANES, wide), 1)
        v = jnp.where((row_ids == col_ids) & (row_ids < rows), F32(-1e30), v)
        s[r, :] = v
        m = jnp.max(v, axis=1, keepdims=True)
        l = jnp.sum(jnp.exp(v - m), axis=1, keepdims=True)
        rstat[0:1, r] = jnp.transpose(jnp.broadcast_to(m, (LANES, LANES)))[0:1, :]
        rstat[1:2, r] = jnp.transpose(jnp.broadcast_to(l, (LANES, LANES)))[0:1, :]
        return jnp.maximum(top, jnp.max(v, axis=0, keepdims=True)), pos

    start = jnp.full((1, wide), -1e30, F32), jnp.zeros((1, wide), F32)
    top, pos = lax.fori_loop(0, tall // LANES, first, start)
    rstat[2:3, :] = jnp.full((1, tall), jnp.sum(pos), F32)

    def second(i, low):
        r = pl.ds(pl.multiple_of(i * LANES, LANES), LANES)
        return low + jnp.sum(jnp.exp(s[r, :] - top), axis=0, keepdims=True)

    low = lax.fori_loop(0, tall // LANES, second, jnp.zeros((1, wide), F32))
    cstat[...] = jnp.zeros(cstat.shape, F32)
    cstat[0:1, :] = top
    cstat[1:2, :] = low


def merge_kernel(mine, other, r0, r1, r2, r3, out, lse_r):
    wide, rows = out.shape[1], lse_r.shape[1] // 4
    side = wide // 2
    theirs = jnp.concatenate([other[:, side:], other[:, :side]], 1)
    m1, m2 = mine[0:1, :], theirs[0:1, :]
    m = jnp.maximum(m1, m2)
    lse = combine((r0, r1, r2, r3), rows)
    lse_r[...] = jnp.broadcast_to(lse, lse_r.shape)
    positive = r0[2:3, 0:1] + r1[2:3, 0:1] + r2[2:3, 0:1] + r3[2:3, 0:1]
    out[...] = jnp.broadcast_to(jnp.sum(lse, axis=1, keepdims=True) - positive, out.shape)
    out[0:1, :] = m
    out[1:2, :] = mine[1:2, :] * jnp.exp(m1 - m) + theirs[1:2, :] * jnp.exp(m2 - m)


def combine(messages, rows):
    groups = messages[0].shape[1] // (4 * rows)
    tops, lows = [], []
    for step, message in zip(ORDER, messages):
        at = [(g * 4 + ORDER.index((k - step) % 4)) * rows for g in range(groups) for k in ORDER]
        tops.append(jnp.concatenate([message[0:1, p : p + rows] for p in at], 1))
        lows.append(jnp.concatenate([message[1:2, p : p + rows] for p in at], 1))
    top = jnp.maximum(jnp.maximum(tops[0], tops[1]), jnp.maximum(tops[2], tops[3]))
    low = sum(l * jnp.exp(t - top) for t, l in zip(tops, lows))
    return top + jnp.log(low)


def weights_kernel(s, mates, lse_r, c0, c1, c2, c3, cols, near, far, part):
    tall, wide = s.shape
    side = wide // 2
    lse_c = combine((c0, c1, c2, c3), tall // 4)
    ids = cols[...]

    @pl.loop(0, tall // LANES)
    def _(i):
        r = pl.ds(pl.multiple_of(i * LANES, LANES), LANES)
        v = s[r, :]
        hit = ids == mates[r, 0:1]
        w = jnp.exp(v - column(lse_r[0:1, r], LANES)) + jnp.exp(v - lse_c)
        w = (w - jnp.where(hit, F32(2.0), F32(0.0))).astype(BF16)
        near[r, :] = w[:, :side]
        far[r, :] = w[:, side:]

    part[...] = c0[2:3, 0:LANES] + c1[2:3, 0:LANES] + c2[2:3, 0:LANES] + c3[2:3, 0:LANES]


def pack(dst, at, g):
    n, w = g.shape
    m = jnp.maximum(jnp.max(jnp.abs(g), axis=1, keepdims=True), F32(1e-30))
    k = jnp.ceil(jnp.log(m) * STEPS)
    q = (g * (LEVELS * jnp.exp(k * (-1.0 / STEPS))) + F32(12582912.0)) - F32(12582912.0)
    dst[at : at + n, 0:w] = q.astype(jnp.int32).astype(I16)
    dst[at : at + n, w : w + LANES] = jnp.broadcast_to(k, (n, LANES)).astype(jnp.int32).astype(I16)


def unpack(src, at, n):
    w = src.shape[1] - LANES
    k = src[at : at + n, w : w + LANES].astype(jnp.int32).astype(F32)[:, :1]
    q = src[at : at + n, 0:w].astype(jnp.int32).astype(F32)
    return q * (jnp.exp(k * (1.0 / STEPS)) * (1.0 / LEVELS))


def hand_out(acc, fwd, bwd, keep1, keep3, own):
    rows = own.shape[0]
    cut = rows // 2
    pack(fwd, 0, acc[3 * rows : 3 * rows + cut, :])
    pack(fwd, cut, acc[rows + cut : 2 * rows, :])
    pack(bwd, 0, acc[3 * rows + cut : 4 * rows, :])
    pack(bwd, cut, acc[2 * rows : 2 * rows + cut, :])
    keep1[...] = acc[rows : rows + cut, :]
    keep3[...] = acc[2 * rows + cut : 3 * rows, :]
    own[...] = acc[0:rows, :]


def z_kernel(near, far, b, o, fwd, bwd, keep1, keep3, own, acc):
    w = acc.shape[1]
    acc[...] = dot(near[...], b[:, :w], NN) + dot(far[...], o[:, :w], NN)
    hand_out(acc, fwd, bwd, keep1, keep3, own)


def x_kernel(near, far, a, o, fwd, bwd, keep1, keep3, own, acc):
    w = a.shape[1] - acc.shape[1]
    acc[...] = dot(near[...], a[:, w:], TN) + dot(far[...], o[...], TN)
    hand_out(acc, fwd, bwd, keep1, keep3, own)


def forward_kernel(fwd, bwd, keep1, keep3, to_up, to_down):
    cut = keep1.shape[0]
    pack(to_up, 0, unpack(fwd, 0, cut) + keep1[...])
    pack(to_down, 0, unpack(bwd, 0, cut) + keep3[...])


def finish_kernel(mult, e, oz, fz, bz, uz, dz, ox, fx, bx, ux, dx, grad):
    cut, half = e.shape[0] // 2, oz.shape[1]
    for h in (0, 1):
        r = slice(h * cut, (h + 1) * cut)
        terms = []
        for own, f, b, u, d in ((oz, fz, bz, uz, dz), (ox, fx, bx, ux, dx)):
            step, straight = (u, b) if h == 0 else (d, f)
            terms.append(own[r, :] + unpack(step, 0, cut) + unpack(straight, cut, cut))
        g0, g1 = mult[0] * terms[0], mult[0] * terms[1]
        e0, e1 = e[r, :half].astype(F32), e[r, half:].astype(F32)
        square = jnp.sum(e0 * e0, axis=1, keepdims=True) + jnp.sum(e1 * e1, axis=1, keepdims=True)
        factor = lax.rsqrt(square + 1e-06)
        inner = jnp.sum(e0 * g0, axis=1, keepdims=True) + jnp.sum(e1 * g1, axis=1, keepdims=True)
        scale = factor * factor * factor * inner
        grad[r, :half] = (factor * g0 - scale * e0).astype(BF16)
        grad[r, half:] = (factor * g1 - scale * e1).astype(BF16)


def local(embeddings, partner, logit_scale):
    rows, width = embeddings.shape
    cut, side = rows // 2, 4 * rows
    total = rows * 2 * X * Z
    c, x, z = lax.axis_index("c"), lax.axis_index("x"), lax.axis_index("z")

    emb = swap(embeddings)
    mate = swap(partner.reshape(1, rows)).reshape(rows, 1)
    digits = jnp.concatenate([mate // 64, mate % 64, jnp.zeros((rows, LANES - 2), jnp.int32)], 1)
    wide = shape(rows, width + LANES, dtype=BF16)
    u, v = call(unit_kernel, "unit", (emb, digits.astype(BF16)), (emb, wide))

    zu, zd, xu, xd = lax.optimization_barrier((up(v, "z"), down(v, "z"), up(u, "x"), down(u, "x")))
    half_z, half_x = shape(cut, width + LANES, dtype=BF16), shape(cut, width, dtype=BF16)
    xa, xb, za, zb = call(
        halves_kernel, "halves", (xu, xd, zu, zd), (half_x, half_x, half_z, half_z)
    )
    xa, xb, za, zb = lax.optimization_barrier(
        (up(xa, "x"), down(xb, "x"), up(za, "z"), down(zb, "z"))
    )
    b = stack("stack", u, xd, xu, xa, xb)
    bo = other_core(b)
    along = {"z": width * 9 // 16, "x": width * 7 // 16}
    flops = 2 * side * side * width
    a, last, mates, early = call(
        early_kernel, "early", (v, zd, zu, za, zb, b),
        (
            shape(side, width, dtype=BF16), shape(side, along["x"], dtype=BF16),
            shape(side, LANES), shape(side, side),
        ),
        flops=flops,
    )
    within = jnp.arange(rows, dtype=jnp.int32)
    cols = jnp.concatenate(
        [((cc * X + (x + k) % X) * Z + z) * rows + within for cc in (c, 1 - c) for k in ORDER]
    ).reshape(1, -1).astype(F32)
    last_other = other_core(after(last, bo))
    scores, rstat, cstat = call(
        tail_kernel, "tail", (logit_scale, a, bo, early, mates, cols),
        (shape(side, 2 * side), shape(8, side), shape(8, 2 * side)), flops=flops,
    )
    cstat_other = other_core(cstat)
    rstats = gather_small(rstat, "z")
    merged, lse_r = call(merge_kernel, "merge", (cstat, cstat_other, *rstats), (cstat, rstat))
    cstats = gather_small(merged, "x")
    near, far, part = call(
        weights_kernel, "weights", (scores, mates, lse_r, *cstats, cols),
        (shape(side, side, dtype=BF16), shape(side, side, dtype=BF16), shape(1, LANES)),
    )
    far_other = other_core(far)

    def sizes(axis):
        w = along[axis]
        message, kept = shape(rows, w + LANES, dtype=I16), shape(cut, w)
        return (
            (message, message, kept, kept, shape(rows, w)),
            dict(scratch=[pltpu.VMEM((side, w), F32)], flops=4 * side * side * w, mib=20),
        )

    outs, options = sizes("z")
    fz, bz, k1z, k3z, oz = call(z_kernel, "along_z", (near, far, b, bo), outs, **options)
    fz, bz = up(fz, "z"), down(bz, "z")
    outs, options = sizes("x")
    fx, bx, k1x, k3x, ox = call(x_kernel, "along_x", (near, far_other, a, last_other), outs, **options)
    fx, bx = up(fx, "x"), down(bx, "x")
    short = {i: shape(cut, w + LANES, dtype=I16) for i, w in along.items()}
    uz, dz = call(forward_kernel, "forward_z", (fz, bz, k1z, k3z), (short["z"],) * 2)
    uz, dz = up(uz, "z"), down(dz, "z")
    ux, dx = call(forward_kernel, "forward_x", (fx, bx, k1x, k3x), (short["x"],) * 2)
    ux, dx = up(ux, "x"), down(dx, "x")
    grad, = call(
        finish_kernel, "finish",
        (logit_scale, emb, oz, fz, bz, uz, dz, ox, fx, bx, ux, dx),
        (shape(rows, width, dtype=BF16),),
    )
    part = after(part, grad)
    both = swap(part) + lax.ppermute(part, ("yl", "c"), SWAP_OTHER)
    return swap(grad), (both[0, :1] / total)


def solution(mesh):
    fine = Mesh(
        mesh.devices.reshape(2, X, Z, 2, 2), ("yl", "x", "z", "yh", "c")
    )
    rows = ("yh", "c", "yl", "x", "z")
    return jax.shard_map(
        local,
        mesh=fine,
        in_specs=(P(rows, None), P(rows), P()),
        out_specs=(P(rows, None), P(("yh", "c"))),
        check_vma=False,
    )
```

```python
import math

import jax
import jax.numpy as jnp
from jax import lax
from jax.experimental import pallas as pl
from jax.experimental.pallas import tpu as pltpu
from jax.sharding import Mesh, PartitionSpec as P

X, Z = 4, 4
ORDER = (0, 1, 3, 2)
LANES = 128
LEVELS = 32000.0
STEPS = 64 / math.log(2.0)
NN = (((1,), (0,)), ((), ()))
NT = (((1,), (1,)), ((), ()))
TN = (((0,), (0,)), ((), ()))
F32, BF16, I16 = jnp.float32, jnp.bfloat16, jnp.int16


def ring(n, step):
    return [(i, (i + step) % n) for i in range(n)]


SWAP = [(0, 0), (1, 2), (2, 1), (3, 3)]
SWAP_OTHER = [(1, 0), (3, 1), (0, 2), (2, 3)]


def swap(v):
    return lax.ppermute(v, ("yl", "c"), SWAP)


def other_core(v):
    return lax.ppermute(v, "c", ring(2, 1))


def up(v, axis):
    return lax.ppermute(v, axis, ring(4, 1))


def down(v, axis):
    return lax.ppermute(v, axis, ring(4, -1))


def after(v, *others):
    return lax.optimization_barrier((v, *others))[0]


def gather_small(v, axis):
    return [v] + [lax.ppermute(v, axis, ring(4, -k)) for k in ORDER[1:]]


def dot(a, b, dims):
    return lax.dot_general(a, b, dims, preferred_element_type=F32)


def call(kernel, name, args, outs, scratch=(), flops=0, mib=14):
    args = [
        pltpu.with_memory_space_constraint(a, pltpu.VMEM) if a.size * a.dtype.itemsize >= 1 << 19 else a
        for a in args
    ]
    vmem = pl.BlockSpec(memory_space=pltpu.VMEM)
    smem = pl.BlockSpec(memory_space=pltpu.SMEM)
    size = sum(a.size * a.dtype.itemsize for a in list(args) + list(outs))
    return pl.pallas_call(
        kernel,
        name=name,
        out_shape=tuple(jax.ShapeDtypeStruct(o.shape, o.dtype) for o in outs),
        in_specs=[smem if a.shape == (1,) else vmem for a in args],
        out_specs=tuple(vmem for _ in outs),
        scratch_shapes=list(scratch),
        cost_estimate=pl.CostEstimate(flops=flops, bytes_accessed=size, transcendentals=0),
        compiler_params=pltpu.CompilerParams(vmem_limit_bytes=mib << 20),
    )(*args)


def shape(*dims, dtype=F32):
    return jax.ShapeDtypeStruct(dims, dtype)


def halves_kernel(xu, xd, zu, zd, xa, xb, za, zb):
    cut = xa.shape[0]
    xa[...] = xu[0:cut, :]
    za[...] = zu[0:cut, :]
    xb[...] = xd[cut:, :]
    zb[...] = zd[cut:, :]


def stack_kernel(*refs):
    at = 0
    for v in refs[:-1]:
        refs[-1][at : at + v.shape[0], :] = v[...]
        at += v.shape[0]


def stack(name, *refs):
    out = shape(sum(r.shape[0] for r in refs), refs[0].shape[1], dtype=BF16)
    return call(stack_kernel, name, refs, (out,))[0]


def unit_kernel(e, digits, u, v, cols):
    rows = e.shape[0]
    c, x, z = lax.axis_index("c"), lax.axis_index("x"), lax.axis_index("z")
    within = lax.broadcasted_iota(jnp.int32, (1, rows), 1)
    for i, cc in enumerate((c, 1 - c)):
        for j, k in enumerate(ORDER):
            first = ((cc * X + lax.rem(x + k, X)) * Z + z) * rows
            at = (4 * i + j) * rows
            cols[:, at : at + rows] = (first + within).astype(F32)
    wide = e[...].astype(F32)
    unit = wide * lax.rsqrt(jnp.sum(wide * wide, axis=1, keepdims=True) + 1e-06)
    u[...] = unit.astype(BF16)
    v[:, : e.shape[1]] = unit.astype(BF16)
    v[:, e.shape[1] :] = digits[...]


def early_kernel(v, zd, zu, za, zb, b, a, last, mates, s):
    width, w = a.shape[1], last.shape[1]
    at = 0
    for r in (v, zd, zu, za, zb):
        n = r.shape[0]
        a[at : at + n, :] = r[:, :width]
        last[at : at + n, :] = r[:, width - w : width]
        two = r[:, width:].astype(F32)
        mates[at : at + n, :] = jnp.broadcast_to(two[:, 0:1] * F32(64.0) + two[:, 1:2], (n, LANES))
        at += n
    s[...] = dot(a[...], b[...], NT)


def column(row, n):
    return jnp.transpose(jnp.broadcast_to(row, (LANES, n)))[:, :1]


def tail_kernel(mult, a, b, early, mates, cols, s, rstat, cstat):
    side, rows = early.shape[0], early.shape[0] // 4
    s[:, 0:side] = early[...]
    s[:, side:] = dot(a[...], b[...], NT)
    multiplier = mult[0]
    tall, wide = s.shape
    rstat[...] = jnp.zeros(rstat.shape, F32)
    ids = cols[...]

    def first(i, carry):
        top, pos = carry
        r = pl.ds(pl.multiple_of(i * LANES, LANES), LANES)
        v = s[r, :] * multiplier
        pos += jnp.sum(jnp.where(ids == mates[r, 0:1], v, F32(0.0)), axis=0, keepdims=True)
        row_ids = i * LANES + lax.broadcasted_iota(jnp.int32, (LANES, wide), 0)
        col_ids = lax.broadcasted_iota(jnp.int32, (LANES, wide), 1)
        v = jnp.where((row_ids == col_ids) & (row_ids < rows), F32(-1e30), v)
        s[r, :] = v
        m = jnp.max(v, axis=1, keepdims=True)
        l = jnp.sum(jnp.exp(v - m), axis=1, keepdims=True)
        rstat[0:1, r] = jnp.transpose(jnp.broadcast_to(m, (LANES, LANES)))[0:1, :]
        rstat[1:2, r] = jnp.transpose(jnp.broadcast_to(l, (LANES, LANES)))[0:1, :]
        return jnp.maximum(top, jnp.max(v, axis=0, keepdims=True)), pos

    start = jnp.full((1, wide), -1e30, F32), jnp.zeros((1, wide), F32)
    top, pos = lax.fori_loop(0, tall // LANES, first, start)
    rstat[2:3, :] = jnp.full((1, tall), jnp.sum(pos), F32)

    def second(i, low):
        r = pl.ds(pl.multiple_of(i * LANES, LANES), LANES)
        return low + jnp.sum(jnp.exp(s[r, :] - top), axis=0, keepdims=True)

    low = lax.fori_loop(0, tall // LANES, second, jnp.zeros((1, wide), F32))
    cstat[...] = jnp.zeros(cstat.shape, F32)
    cstat[0:1, :] = top
    cstat[1:2, :] = low


def merge_kernel(mine, other, r0, r1, r2, r3, out, lse_r):
    wide, rows = out.shape[1], lse_r.shape[1] // 4
    side = wide // 2
    theirs = jnp.concatenate([other[:, side:], other[:, :side]], 1)
    m1, m2 = mine[0:1, :], theirs[0:1, :]
    m = jnp.maximum(m1, m2)
    lse = combine((r0, r1, r2, r3), rows)
    lse_r[...] = jnp.broadcast_to(lse, lse_r.shape)
    positive = r0[2:3, 0:1] + r1[2:3, 0:1] + r2[2:3, 0:1] + r3[2:3, 0:1]
    out[...] = jnp.broadcast_to(jnp.sum(lse, axis=1, keepdims=True) - positive, out.shape)
    out[0:1, :] = m
    out[1:2, :] = mine[1:2, :] * jnp.exp(m1 - m) + theirs[1:2, :] * jnp.exp(m2 - m)


def combine(messages, rows):
    groups = messages[0].shape[1] // (4 * rows)
    tops, lows = [], []
    for step, message in zip(ORDER, messages):
        at = [(g * 4 + ORDER.index((k - step) % 4)) * rows for g in range(groups) for k in ORDER]
        tops.append(jnp.concatenate([message[0:1, p : p + rows] for p in at], 1))
        lows.append(jnp.concatenate([message[1:2, p : p + rows] for p in at], 1))
    top = jnp.maximum(jnp.maximum(tops[0], tops[1]), jnp.maximum(tops[2], tops[3]))
    low = sum(l * jnp.exp(t - top) for t, l in zip(tops, lows))
    return top + jnp.log(low)


def weights_kernel(s, mates, lse_r, c0, c1, c2, c3, cols, near, far, part):
    tall, wide = s.shape
    side = wide // 2
    lse_c = combine((c0, c1, c2, c3), tall // 4)
    ids = cols[...]

    @pl.loop(0, tall // LANES)
    def _(i):
        r = pl.ds(pl.multiple_of(i * LANES, LANES), LANES)
        v = s[r, :]
        hit = ids == mates[r, 0:1]
        w = jnp.exp(v - column(lse_r[0:1, r], LANES)) + jnp.exp(v - lse_c)
        w = (w - jnp.where(hit, F32(2.0), F32(0.0))).astype(BF16)
        near[r, :] = w[:, :side]
        far[r, :] = w[:, side:]

    part[...] = c0[2:3, 0:LANES] + c1[2:3, 0:LANES] + c2[2:3, 0:LANES] + c3[2:3, 0:LANES]


def pack(dst, at, g):
    n, w = g.shape
    m = jnp.maximum(jnp.max(jnp.abs(g), axis=1, keepdims=True), F32(1e-30))
    k = jnp.ceil(jnp.log(m) * STEPS)
    q = (g * (LEVELS * jnp.exp(k * (-1.0 / STEPS))) + F32(12582912.0)) - F32(12582912.0)
    dst[at : at + n, 0:w] = q.astype(jnp.int32).astype(I16)
    dst[at : at + n, w : w + LANES] = jnp.broadcast_to(k, (n, LANES)).astype(jnp.int32).astype(I16)


def unpack(src, at, n):
    w = src.shape[1] - LANES
    k = src[at : at + n, w : w + LANES].astype(jnp.int32).astype(F32)[:, :1]
    q = src[at : at + n, 0:w].astype(jnp.int32).astype(F32)
    return q * (jnp.exp(k * (1.0 / STEPS)) * (1.0 / LEVELS))


def hand_out(acc, late_fwd, late_bwd, keep1, keep3, own):
    rows = own.shape[0]
    cut = rows // 2
    pack(late_fwd, 0, acc[rows + cut : 2 * rows, :])
    pack(late_bwd, 0, acc[2 * rows : 2 * rows + cut, :])
    keep1[...] = acc[rows : rows + cut, :]
    keep3[...] = acc[2 * rows + cut : 3 * rows, :]
    own[...] = acc[0:rows, :]


def z_first_kernel(near, far, b, o, fwd, bwd, acc):
    n, w = acc.shape
    r = slice(near.shape[0] - n, None)
    acc[...] = dot(near[r, :], b[:, :w], NN) + dot(far[r, :], o[:, :w], NN)
    pack(fwd, 0, acc[0 : n // 2, :])
    pack(bwd, 0, acc[n // 2 :, :])


def z_kernel(near, far, b, o, late_fwd, late_bwd, keep1, keep3, own, acc):
    n, w = acc.shape
    acc[...] = dot(near[0:n, :], b[:, :w], NN) + dot(far[0:n, :], o[:, :w], NN)
    hand_out(acc, late_fwd, late_bwd, keep1, keep3, own)


def x_first_kernel(near, far, a, o, fwd, bwd, acc):
    n, w = acc.shape[0], a.shape[1] - acc.shape[1]
    r = slice(near.shape[1] - n, None)
    acc[...] = dot(near[:, r], a[:, w:], TN) + dot(far[:, r], o[...], TN)
    pack(fwd, 0, acc[0 : n // 2, :])
    pack(bwd, 0, acc[n // 2 :, :])


def x_kernel(near, far, a, o, late_fwd, late_bwd, keep1, keep3, own, acc):
    n, w = acc.shape[0], a.shape[1] - acc.shape[1]
    acc[...] = dot(near[:, 0:n], a[:, w:], TN) + dot(far[:, 0:n], o[...], TN)
    hand_out(acc, late_fwd, late_bwd, keep1, keep3, own)


def forward_kernel(fwd, bwd, late_fwd, late_bwd, keep1, keep3, to_up, to_down):
    cut = keep1.shape[0]
    pack(to_up, 0, unpack(fwd, 0, cut) + keep1[...])
    pack(to_down, 0, unpack(bwd, 0, cut) + keep3[...])
    to_up[cut:, :] = late_fwd[...]
    to_down[cut:, :] = late_bwd[...]


def finish_kernel(mult, e, oz, uz, dz, ox, ux, dx, grad):
    cut, half = e.shape[0] // 2, oz.shape[1]
    for h in (0, 1):
        r = slice(h * cut, (h + 1) * cut)
        terms = []
        for own, u, d in ((oz, uz, dz), (ox, ux, dx)):
            step, straight = (u, d) if h == 0 else (d, u)
            terms.append(own[r, :] + unpack(step, 0, cut) + unpack(straight, cut, cut))
        g0, g1 = mult[0] * terms[0], mult[0] * terms[1]
        e0, e1 = e[r, :half].astype(F32), e[r, half:].astype(F32)
        square = jnp.sum(e0 * e0, axis=1, keepdims=True) + jnp.sum(e1 * e1, axis=1, keepdims=True)
        factor = lax.rsqrt(square + 1e-06)
        inner = jnp.sum(e0 * g0, axis=1, keepdims=True) + jnp.sum(e1 * g1, axis=1, keepdims=True)
        scale = factor * factor * factor * inner
        grad[r, :half] = (factor * g0 - scale * e0).astype(BF16)
        grad[r, half:] = (factor * g1 - scale * e1).astype(BF16)


def local(embeddings, partner, logit_scale):
    rows, width = embeddings.shape
    cut, side = rows // 2, 4 * rows
    total = rows * 2 * X * Z

    emb = swap(embeddings)
    mate = swap(partner.reshape(1, rows)).reshape(rows, 1)
    digits = jnp.concatenate([mate // 64, mate % 64, jnp.zeros((rows, LANES - 2), jnp.int32)], 1)
    wide = shape(rows, width + LANES, dtype=BF16)
    u, v, cols = call(
        unit_kernel, "unit", (emb, digits.astype(BF16)), (emb, wide, shape(1, 2 * side))
    )

    zu, zd, xu, xd = lax.optimization_barrier((up(v, "z"), down(v, "z"), up(u, "x"), down(u, "x")))
    half_z, half_x = shape(cut, width + LANES, dtype=BF16), shape(cut, width, dtype=BF16)
    xa, xb, za, zb = call(
        halves_kernel, "halves", (xu, xd, zu, zd), (half_x, half_x, half_z, half_z)
    )
    xa, xb, za, zb = lax.optimization_barrier(
        (up(xa, "x"), down(xb, "x"), up(za, "z"), down(zb, "z"))
    )
    b = stack("stack", u, xd, xu, xa, xb)
    bo = other_core(b)
    along = {"z": width * 9 // 16, "x": width * 7 // 16}
    flops = 2 * side * side * width
    a, last, mates, early = call(
        early_kernel, "early", (v, zd, zu, za, zb, b),
        (
            shape(side, width, dtype=BF16), shape(side, along["x"], dtype=BF16),
            shape(side, LANES), shape(side, side),
        ),
        flops=flops,
    )
    last_other = other_core(after(last, bo))
    scores, rstat, cstat = call(
        tail_kernel, "tail", (logit_scale, a, bo, early, mates, cols),
        (shape(side, 2 * side), shape(8, side), shape(8, 2 * side)), flops=flops,
    )
    cstat_other = other_core(cstat)
    rstats = gather_small(rstat, "z")
    merged, lse_r = call(merge_kernel, "merge", (cstat, cstat_other, *rstats), (cstat, rstat))
    cstats = gather_small(merged, "x")
    near, far, part = call(
        weights_kernel, "weights", (scores, mates, lse_r, *cstats, cols),
        (shape(side, side, dtype=BF16), shape(side, side, dtype=BF16), shape(1, LANES)),
    )
    far_other = other_core(far)

    def terms(kernels, axis, operands):
        w = along[axis]
        message, kept = shape(cut, w + LANES, dtype=I16), shape(cut, w)
        flops = 4 * side * rows * w
        first = lambda *o: call(
            kernels[0], "first_" + axis, o, (message, message),
            scratch=[pltpu.VMEM((rows, w), F32)], flops=flops,
        )
        rest = lambda *o: call(
            kernels[1], "rest_" + axis, o, (message, message, kept, kept, shape(rows, w)),
            scratch=[pltpu.VMEM((3 * rows, w), F32)], flops=3 * flops, mib=18,
        )
        return first(*operands), rest

    operands_z, operands_x = (near, far, b, bo), (near, far_other, a, last_other)
    (fz, bz), rest_z = terms((z_first_kernel, z_kernel), "z", operands_z)
    (fx, bx), rest_x = terms((x_first_kernel, x_kernel), "x", operands_x)
    *kept_z, oz = rest_z(after(near, fx), *operands_z[1:])
    *kept_x, ox = rest_x(after(near, oz), *operands_x[1:])
    fz, bz = up(fz, "z"), down(bz, "z")
    fx, bx = up(fx, "x"), down(bx, "x")
    message = {i: shape(rows, w + LANES, dtype=I16) for i, w in along.items()}
    uz, dz = call(forward_kernel, "forward_z", (fz, bz, *kept_z), (message["z"],) * 2)
    uz, dz = up(uz, "z"), down(dz, "z")
    ux, dx = call(forward_kernel, "forward_x", (fx, bx, *kept_x), (message["x"],) * 2)
    ux, dx = up(ux, "x"), down(dx, "x")
    grad, = call(
        finish_kernel, "finish",
        (logit_scale, emb, oz, uz, dz, ox, ux, dx),
        (shape(rows, width, dtype=BF16),),
    )
    part = after(part, grad)
    both = swap(part) + lax.ppermute(part, ("yl", "c"), SWAP_OTHER)
    return swap(grad), (both[0, :1] / total)


def solution(mesh):
    fine = Mesh(
        mesh.devices.reshape(2, X, Z, 2, 2), ("yl", "x", "z", "yh", "c")
    )
    rows = ("yh", "c", "yl", "x", "z")
    return jax.shard_map(
        local,
        mesh=fine,
        in_specs=(P(rows, None), P(rows), P()),
        out_specs=(P(rows, None), P(("yh", "c"))),
        check_vma=False,
    )
```

```python
import math

import jax
import jax.numpy as jnp
from jax import lax
from jax.experimental import pallas as pl
from jax.experimental.pallas import tpu as pltpu
from jax.sharding import Mesh, PartitionSpec as P

X, Z = 4, 4
ORDER = (0, 1, 3, 2)
LANES = 128
LEVELS = 32000.0
STEPS = 64 / math.log(2.0)
NN = (((1,), (0,)), ((), ()))
NT = (((1,), (1,)), ((), ()))
TN = (((0,), (0,)), ((), ()))
F32, BF16, I16 = jnp.float32, jnp.bfloat16, jnp.int16


def ring(n, step):
    return [(i, (i + step) % n) for i in range(n)]


SWAP = [(0, 0), (1, 2), (2, 1), (3, 3)]
SWAP_OTHER = [(1, 0), (3, 1), (0, 2), (2, 3)]


def swap(v):
    return lax.ppermute(v, ("yl", "c"), SWAP)


def other_core(v):
    return lax.ppermute(v, "c", ring(2, 1))


def up(v, axis):
    return lax.ppermute(v, axis, ring(4, 1))


def down(v, axis):
    return lax.ppermute(v, axis, ring(4, -1))


def after(v, *others):
    return lax.optimization_barrier((v, *others))[0]


def gather_small(v, axis):
    return [v] + [lax.ppermute(v, axis, ring(4, -k)) for k in ORDER[1:]]


def dot(a, b, dims):
    return lax.dot_general(a, b, dims, preferred_element_type=F32)


def call(kernel, name, args, outs, scratch=(), flops=0, mib=14):
    args = [
        pltpu.with_memory_space_constraint(a, pltpu.VMEM) if a.size * a.dtype.itemsize >= 1 << 19 else a
        for a in args
    ]
    vmem = pl.BlockSpec(memory_space=pltpu.VMEM)
    smem = pl.BlockSpec(memory_space=pltpu.SMEM)
    size = sum(a.size * a.dtype.itemsize for a in list(args) + list(outs))
    return pl.pallas_call(
        kernel,
        name=name,
        out_shape=tuple(jax.ShapeDtypeStruct(o.shape, o.dtype) for o in outs),
        in_specs=[smem if a.shape == (1,) else vmem for a in args],
        out_specs=tuple(vmem for _ in outs),
        scratch_shapes=list(scratch),
        cost_estimate=pl.CostEstimate(flops=flops, bytes_accessed=size, transcendentals=0),
        compiler_params=pltpu.CompilerParams(vmem_limit_bytes=mib << 20),
    )(*args)


def shape(*dims, dtype=F32):
    return jax.ShapeDtypeStruct(dims, dtype)


def halves_kernel(xu, xd, zu, zd, xa, xb, za, zb):
    cut = xa.shape[0]
    xa[...] = xu[0:cut, :]
    za[...] = zu[0:cut, :]
    xb[...] = xd[cut:, :]
    zb[...] = zd[cut:, :]


def stack_kernel(*refs):
    at = 0
    for v in refs[:-1]:
        refs[-1][at : at + v.shape[0], :] = v[...]
        at += v.shape[0]


def stack(name, *refs):
    out = shape(sum(r.shape[0] for r in refs), refs[0].shape[1], dtype=BF16)
    return call(stack_kernel, name, refs, (out,))[0]


def unit_kernel(e, digits, u, v, cols):
    rows = e.shape[0]
    c, x, z = lax.axis_index("c"), lax.axis_index("x"), lax.axis_index("z")
    within = lax.broadcasted_iota(jnp.int32, (1, rows), 1)
    for i, cc in enumerate((c, 1 - c)):
        for j, k in enumerate(ORDER):
            first = ((cc * X + lax.rem(x + k, X)) * Z + z) * rows
            at = (4 * i + j) * rows
            cols[:, at : at + rows] = (first + within).astype(F32)
    wide = e[...].astype(F32)
    unit = wide * lax.rsqrt(jnp.sum(wide * wide, axis=1, keepdims=True) + 1e-06)
    u[...] = unit.astype(BF16)
    v[:, : e.shape[1]] = unit.astype(BF16)
    v[:, e.shape[1] :] = digits[...]


def statistics(s, ids, mates, multiplier, own, rstat, cstat):
    tall, wide = s.shape

    def first(i, carry):
        top, pos = carry
        r = pl.ds(pl.multiple_of(i * LANES, LANES), LANES)
        v = s[r, :] * multiplier
        pos += jnp.sum(jnp.where(ids == mates[r, 0:1], v, F32(0.0)), axis=0, keepdims=True)
        if own:
            row_ids = i * LANES + lax.broadcasted_iota(jnp.int32, (LANES, wide), 0)
            col_ids = lax.broadcasted_iota(jnp.int32, (LANES, wide), 1)
            v = jnp.where((row_ids == col_ids) & (row_ids < tall // 4), F32(-1e30), v)
        s[r, :] = v
        m = jnp.max(v, axis=1, keepdims=True)
        l = jnp.sum(jnp.exp(v - m), axis=1, keepdims=True)
        rstat[0:1, r] = jnp.transpose(jnp.broadcast_to(m, (LANES, LANES)))[0:1, :]
        rstat[1:2, r] = jnp.transpose(jnp.broadcast_to(l, (LANES, LANES)))[0:1, :]
        return jnp.maximum(top, jnp.max(v, axis=0, keepdims=True)), pos

    start = jnp.full((1, wide), -1e30, F32), jnp.zeros((1, wide), F32)
    top, pos = lax.fori_loop(0, tall // LANES, first, start)

    def second(i, low):
        r = pl.ds(pl.multiple_of(i * LANES, LANES), LANES)
        return low + jnp.sum(jnp.exp(s[r, :] - top), axis=0, keepdims=True)

    cstat[0:1, :] = top
    cstat[1:2, :] = lax.fori_loop(0, tall // LANES, second, jnp.zeros((1, wide), F32))
    cstat[2:3, :] = pos


def near_kernel(v, zd, zu, b, bo, s1, s2, a):
    at = 0
    for r in (v, zd, zu):
        a[at : at + r.shape[0], :] = r[:, : a.shape[1]]
        at += r.shape[0]
    s1[...] = dot(a[...], b[...], NT)
    s2[...] = dot(a[...], bo[...], NT)


def complete(s, known, a, b, t):
    n = known.shape[0]
    s[0:n, 0:n] = known[...]
    s[n:, 0:n] = dot(a[n:, :], b[...], NT)
    s[:, n:] = dot(a[...], t[...], NT)


def early_kernel(mult, v, zd, zu, za, zb, b, t, known, cols, a, last, mates, s, rstat, cstat):
    width, w = a.shape[1], last.shape[1]
    at = 0
    for r in (v, zd, zu, za, zb):
        n = r.shape[0]
        a[at : at + n, :] = r[:, :width]
        last[at : at + n, :] = r[:, width - w : width]
        two = r[:, width:].astype(F32)
        mates[at : at + n, :] = jnp.broadcast_to(two[:, 0:1] * F32(64.0) + two[:, 1:2], (n, LANES))
        at += n
    complete(s, known, a, b, t)
    rstat[...] = jnp.zeros(rstat.shape, F32)
    cstat[...] = jnp.zeros(cstat.shape, F32)
    statistics(s, cols[:, : s.shape[1]], mates, mult[0], True, rstat, cstat)


def column(row, n):
    return jnp.transpose(jnp.broadcast_to(row, (LANES, n)))[:, :1]


def tail_kernel(mult, a, b, t, known, mates, cols, rs1, cs1, s, rstat, cstat, rs2, cs2):
    side = s.shape[1]
    complete(s, known, a, b, t)
    statistics(s, cols[:, side:], mates, mult[0], False, rs2, cs2)
    m1, m2 = rs1[0:1, :], rs2[0:1, :]
    m = jnp.maximum(m1, m2)
    positive = jnp.sum(cs1[2:3, :] + cs2[2:3, :], axis=1, keepdims=True)
    rstat[...] = jnp.broadcast_to(positive, rstat.shape)
    rstat[0:1, :] = m
    rstat[1:2, :] = rs1[1:2, :] * jnp.exp(m1 - m) + rs2[1:2, :] * jnp.exp(m2 - m)
    cstat[:, 0:side] = cs1[...]
    cstat[:, side:] = cs2[...]


def merge_kernel(mine, other, r0, r1, r2, r3, out, lse_r):
    wide, rows = out.shape[1], lse_r.shape[1] // 4
    side = wide // 2
    theirs = jnp.concatenate([other[:, side:], other[:, :side]], 1)
    m1, m2 = mine[0:1, :], theirs[0:1, :]
    m = jnp.maximum(m1, m2)
    lse = combine((r0, r1, r2, r3), rows)
    lse_r[...] = jnp.broadcast_to(lse, lse_r.shape)
    positive = r0[2:3, 0:1] + r1[2:3, 0:1] + r2[2:3, 0:1] + r3[2:3, 0:1]
    out[...] = jnp.broadcast_to(jnp.sum(lse, axis=1, keepdims=True) - positive, out.shape)
    out[0:1, :] = m
    out[1:2, :] = mine[1:2, :] * jnp.exp(m1 - m) + theirs[1:2, :] * jnp.exp(m2 - m)


def combine(messages, rows):
    groups = messages[0].shape[1] // (4 * rows)
    tops, lows = [], []
    for step, message in zip(ORDER, messages):
        at = [(g * 4 + ORDER.index((k - step) % 4)) * rows for g in range(groups) for k in ORDER]
        tops.append(jnp.concatenate([message[0:1, p : p + rows] for p in at], 1))
        lows.append(jnp.concatenate([message[1:2, p : p + rows] for p in at], 1))
    top = jnp.maximum(jnp.maximum(tops[0], tops[1]), jnp.maximum(tops[2], tops[3]))
    low = sum(l * jnp.exp(t - top) for t, l in zip(tops, lows))
    return top + jnp.log(low)


def weights_kernel(s1, s2, mates, lse_r, c0, c1, c2, c3, cols, near, far, part):
    tall, side = s1.shape
    lse_c = combine((c0, c1, c2, c3), tall // 4)
    ids = cols[...]

    @pl.loop(0, tall // LANES)
    def _(i):
        r = pl.ds(pl.multiple_of(i * LANES, LANES), LANES)
        mate, lse = mates[r, 0:1], column(lse_r[0:1, r], LANES)
        for s, out, at in ((s1, near, 0), (s2, far, side)):
            v = s[r, :]
            w = jnp.exp(v - lse) + jnp.exp(v - lse_c[:, at : at + side])
            hit = ids[:, at : at + side] == mate
            out[r, :] = (w - jnp.where(hit, F32(2.0), F32(0.0))).astype(BF16)

    part[...] = c0[2:3, 0:LANES] + c1[2:3, 0:LANES] + c2[2:3, 0:LANES] + c3[2:3, 0:LANES]


def pack(dst, at, g):
    n, w = g.shape
    m = jnp.maximum(jnp.max(jnp.abs(g), axis=1, keepdims=True), F32(1e-30))
    k = jnp.ceil(jnp.log(m) * STEPS)
    q = (g * (LEVELS * jnp.exp(k * (-1.0 / STEPS))) + F32(12582912.0)) - F32(12582912.0)
    dst[at : at + n, 0:w] = q.astype(jnp.int32).astype(I16)
    dst[at : at + n, w : w + LANES] = jnp.broadcast_to(k, (n, LANES)).astype(jnp.int32).astype(I16)


def unpack(src, at, n):
    w = src.shape[1] - LANES
    k = src[at : at + n, w : w + LANES].astype(jnp.int32).astype(F32)[:, :1]
    q = src[at : at + n, 0:w].astype(jnp.int32).astype(F32)
    return q * (jnp.exp(k * (1.0 / STEPS)) * (1.0 / LEVELS))


def hand_out(acc, late_fwd, late_bwd, keep1, keep3, own):
    rows = own.shape[0]
    cut = rows // 2
    pack(late_fwd, 0, acc[rows + cut : 2 * rows, :])
    pack(late_bwd, 0, acc[2 * rows : 2 * rows + cut, :])
    keep1[...] = acc[rows : rows + cut, :]
    keep3[...] = acc[2 * rows + cut : 3 * rows, :]
    own[...] = acc[0:rows, :]


def z_terms(near, far, r, w, b, t, bo, to):
    n = b.shape[0]
    return (
        dot(near[r, 0:n], b[:, :w], NN)
        + dot(near[r, n:], t[:, :w], NN)
        + dot(far[r, 0:n], bo[:, :w], NN)
        + dot(far[r, n:], to[:, :w], NN)
    )


def z_first_kernel(near, far, b, t, bo, to, fwd, bwd, acc):
    n, w = acc.shape
    r = slice(near.shape[0] - n, None)
    acc[...] = z_terms(near, far, r, w, b, t, bo, to)
    pack(fwd, 0, acc[0 : n // 2, :])
    pack(bwd, 0, acc[n // 2 :, :])


def z_kernel(near, far, b, t, bo, to, late_fwd, late_bwd, keep1, keep3, own, acc):
    n, w = acc.shape
    acc[...] = z_terms(near, far, slice(0, n), w, b, t, bo, to)
    hand_out(acc, late_fwd, late_bwd, keep1, keep3, own)


def x_first_kernel(near, far, a, o, fwd, bwd, acc):
    n, w = acc.shape[0], a.shape[1] - acc.shape[1]
    r = slice(near.shape[1] - n, None)
    acc[...] = dot(near[:, r], a[:, w:], TN) + dot(far[:, r], o[...], TN)
    pack(fwd, 0, acc[0 : n // 2, :])
    pack(bwd, 0, acc[n // 2 :, :])


def x_kernel(near, far, a, o, late_fwd, late_bwd, keep1, keep3, own, acc):
    n, w = acc.shape[0], a.shape[1] - acc.shape[1]
    acc[...] = dot(near[:, 0:n], a[:, w:], TN) + dot(far[:, 0:n], o[...], TN)
    hand_out(acc, late_fwd, late_bwd, keep1, keep3, own)


def forward_kernel(fwd, bwd, late_fwd, late_bwd, keep1, keep3, to_up, to_down):
    cut = keep1.shape[0]
    pack(to_up, 0, unpack(fwd, 0, cut) + keep1[...])
    pack(to_down, 0, unpack(bwd, 0, cut) + keep3[...])
    to_up[cut:, :] = late_fwd[...]
    to_down[cut:, :] = late_bwd[...]


def finish_kernel(mult, e, oz, uz, dz, ox, ux, dx, grad):
    cut, half = e.shape[0] // 2, oz.shape[1]
    for h in (0, 1):
        r = slice(h * cut, (h + 1) * cut)
        terms = []
        for own, u, d in ((oz, uz, dz), (ox, ux, dx)):
            step, straight = (u, d) if h == 0 else (d, u)
            terms.append(own[r, :] + unpack(step, 0, cut) + unpack(straight, cut, cut))
        g0, g1 = mult[0] * terms[0], mult[0] * terms[1]
        e0, e1 = e[r, :half].astype(F32), e[r, half:].astype(F32)
        square = jnp.sum(e0 * e0, axis=1, keepdims=True) + jnp.sum(e1 * e1, axis=1, keepdims=True)
        factor = lax.rsqrt(square + 1e-06)
        inner = jnp.sum(e0 * g0, axis=1, keepdims=True) + jnp.sum(e1 * g1, axis=1, keepdims=True)
        scale = factor * factor * factor * inner
        grad[r, :half] = (factor * g0 - scale * e0).astype(BF16)
        grad[r, half:] = (factor * g1 - scale * e1).astype(BF16)


def local(embeddings, partner, logit_scale):
    rows, width = embeddings.shape
    cut, side = rows // 2, 4 * rows
    total = rows * 2 * X * Z

    emb = swap(embeddings)
    mate = swap(partner.reshape(1, rows)).reshape(rows, 1)
    digits = jnp.concatenate([mate // 64, mate % 64, jnp.zeros((rows, LANES - 2), jnp.int32)], 1)
    wide = shape(rows, width + LANES, dtype=BF16)
    u, v, cols = call(
        unit_kernel, "unit", (emb, digits.astype(BF16)), (emb, wide, shape(1, 2 * side))
    )

    zu, zd, xu, xd = lax.optimization_barrier((up(v, "z"), down(v, "z"), up(u, "x"), down(u, "x")))
    half_z, half_x = shape(cut, width + LANES, dtype=BF16), shape(cut, width, dtype=BF16)
    xa, xb, za, zb = call(
        halves_kernel, "halves", (xu, xd, zu, zd), (half_x, half_x, half_z, half_z)
    )
    b = stack("stack_b", u, xd, xu)
    bo = other_core(b)
    n = b.shape[0]
    known1, known2 = call(
        near_kernel, "near", (v, zd, zu, b, bo), (shape(n, n), shape(n, n)),
        scratch=[pltpu.VMEM((n, width), BF16)], flops=4 * n * n * width,
    )
    xa, xb, za, zb, known1, known2 = lax.optimization_barrier(
        (up(xa, "x"), down(xb, "x"), up(za, "z"), down(zb, "z"), known1, known2)
    )
    t = stack("stack_t", xa, xb)
    to = other_core(t)
    along = {"z": width * 9 // 16, "x": width * 7 // 16}
    flops = 2 * side * side * width
    a, last, mates, near, rstat, cstat = call(
        early_kernel, "early", (logit_scale, v, zd, zu, za, zb, b, t, known1, cols),
        (
            shape(side, width, dtype=BF16), shape(side, along["x"], dtype=BF16),
            shape(side, LANES), shape(side, side), shape(8, side), shape(8, side),
        ),
        flops=flops,
    )
    last_other = other_core(after(last, to))
    far, rstat, cstat = call(
        tail_kernel, "tail", (logit_scale, a, bo, to, known2, mates, cols, rstat, cstat),
        (shape(side, side), shape(8, side), shape(8, 2 * side)),
        scratch=[pltpu.VMEM((8, side), F32), pltpu.VMEM((8, side), F32)], flops=flops,
    )
    cstat_other = other_core(cstat)
    rstats = gather_small(rstat, "z")
    merged, lse_r = call(merge_kernel, "merge", (cstat, cstat_other, *rstats), (cstat, rstat))
    cstats = gather_small(merged, "x")
    near, far, part = call(
        weights_kernel, "weights", (near, far, mates, lse_r, *cstats, cols),
        (shape(side, side, dtype=BF16), shape(side, side, dtype=BF16), shape(1, LANES)),
    )
    far_other = other_core(far)

    def terms(kernels, axis, operands):
        w = along[axis]
        message, kept = shape(cut, w + LANES, dtype=I16), shape(cut, w)
        flops = 4 * side * rows * w
        first = lambda *o: call(
            kernels[0], "first_" + axis, o, (message, message),
            scratch=[pltpu.VMEM((rows, w), F32)], flops=flops,
        )
        rest = lambda *o: call(
            kernels[1], "rest_" + axis, o, (message, message, kept, kept, shape(rows, w)),
            scratch=[pltpu.VMEM((3 * rows, w), F32)], flops=3 * flops, mib=18,
        )
        return first(*operands), rest

    operands_z, operands_x = (near, far, b, t, bo, to), (near, far_other, a, last_other)
    (fz, bz), rest_z = terms((z_first_kernel, z_kernel), "z", operands_z)
    (fx, bx), rest_x = terms((x_first_kernel, x_kernel), "x", operands_x)
    *kept_z, oz = rest_z(after(near, fx), *operands_z[1:])
    *kept_x, ox = rest_x(after(near, oz), *operands_x[1:])
    fz, bz, _ = lax.optimization_barrier((up(fz, "z"), down(bz, "z"), ox))
    fx, bx = up(fx, "x"), down(bx, "x")
    message = {i: shape(rows, w + LANES, dtype=I16) for i, w in along.items()}
    uz, dz = call(forward_kernel, "forward_z", (fz, bz, *kept_z), (message["z"],) * 2)
    uz, dz = up(uz, "z"), down(dz, "z")
    ux, dx = call(forward_kernel, "forward_x", (fx, bx, *kept_x), (message["x"],) * 2)
    ux, dx = up(ux, "x"), down(dx, "x")
    grad, = call(
        finish_kernel, "finish",
        (logit_scale, emb, oz, uz, dz, ox, ux, dx),
        (shape(rows, width, dtype=BF16),),
    )
    part = after(part, grad)
    both = swap(part) + lax.ppermute(part, ("yl", "c"), SWAP_OTHER)
    return swap(grad), (both[0, :1] / total)


def solution(mesh):
    fine = Mesh(
        mesh.devices.reshape(2, X, Z, 2, 2), ("yl", "x", "z", "yh", "c")
    )
    rows = ("yh", "c", "yl", "x", "z")
    return jax.shard_map(
        local,
        mesh=fine,
        in_specs=(P(rows, None), P(rows), P()),
        out_specs=(P(rows, None), P(("yh", "c"))),
        check_vma=False,
    )
```

```python
import math

import jax
import jax.numpy as jnp
from jax import lax
from jax.experimental import pallas as pl
from jax.experimental.pallas import tpu as pltpu
from jax.sharding import Mesh, PartitionSpec as P

X, Z = 4, 4
ORDER = (0, 1, 3, 2)
LANES = 128
LEVELS = 32000.0
STEPS = 64 / math.log(2.0)
NN = (((1,), (0,)), ((), ()))
NT = (((1,), (1,)), ((), ()))
TN = (((0,), (0,)), ((), ()))
F32, BF16, I16 = jnp.float32, jnp.bfloat16, jnp.int16


def ring(n, step):
    return [(i, (i + step) % n) for i in range(n)]


SWAP = [(0, 0), (1, 2), (2, 1), (3, 3)]
SWAP_OTHER = [(1, 0), (3, 1), (0, 2), (2, 3)]


def swap(v):
    return lax.ppermute(v, ("yl", "c"), SWAP)


def other_core(v):
    return lax.ppermute(v, "c", ring(2, 1))


def up(v, axis):
    return lax.ppermute(v, axis, ring(4, 1))


def down(v, axis):
    return lax.ppermute(v, axis, ring(4, -1))


def after(v, *others):
    return lax.optimization_barrier((v, *others))[0]


def gather_small(v, axis):
    return [v] + [lax.ppermute(v, axis, ring(4, -k)) for k in ORDER[1:]]


def dot(a, b, dims):
    return lax.dot_general(a, b, dims, preferred_element_type=F32)


def call(kernel, name, args, outs, scratch=(), flops=0, mib=14):
    args = [
        pltpu.with_memory_space_constraint(a, pltpu.VMEM) if a.size * a.dtype.itemsize >= 1 << 19 else a
        for a in args
    ]
    vmem = pl.BlockSpec(memory_space=pltpu.VMEM)
    smem = pl.BlockSpec(memory_space=pltpu.SMEM)
    size = sum(a.size * a.dtype.itemsize for a in list(args) + list(outs))
    return pl.pallas_call(
        kernel,
        name=name,
        out_shape=tuple(jax.ShapeDtypeStruct(o.shape, o.dtype) for o in outs),
        in_specs=[smem if a.shape == (1,) else vmem for a in args],
        out_specs=tuple(vmem for _ in outs),
        scratch_shapes=list(scratch),
        cost_estimate=pl.CostEstimate(flops=flops, bytes_accessed=size, transcendentals=0),
        compiler_params=pltpu.CompilerParams(vmem_limit_bytes=mib << 20),
    )(*args)


def shape(*dims, dtype=F32):
    return jax.ShapeDtypeStruct(dims, dtype)


def halves_kernel(xu, xd, zu, zd, xa, xb, za, zb):
    cut = xa.shape[0]
    xa[...] = xu[0:cut, :]
    za[...] = zu[0:cut, :]
    xb[...] = xd[cut:, :]
    zb[...] = zd[cut:, :]


def stack_kernel(*refs):
    at = 0
    for v in refs[:-1]:
        refs[-1][at : at + v.shape[0], :] = v[...]
        at += v.shape[0]


def stack(name, *refs):
    out = shape(sum(r.shape[0] for r in refs), refs[0].shape[1], dtype=BF16)
    return call(stack_kernel, name, refs, (out,))[0]


def unit_kernel(e, digits, u, v, cols):
    rows = e.shape[0]
    c, x, z = lax.axis_index("c"), lax.axis_index("x"), lax.axis_index("z")
    within = lax.broadcasted_iota(jnp.int32, (1, rows), 1)
    for i, cc in enumerate((c, 1 - c)):
        for j, k in enumerate(ORDER):
            first = ((cc * X + lax.rem(x + k, X)) * Z + z) * rows
            at = (4 * i + j) * rows
            cols[:, at : at + rows] = (first + within).astype(F32)
    wide = e[...].astype(F32)
    unit = wide * lax.rsqrt(jnp.sum(wide * wide, axis=1, keepdims=True) + 1e-06)
    u[...] = unit.astype(BF16)
    v[:, : e.shape[1]] = unit.astype(BF16)
    v[:, e.shape[1] :] = digits[...]


def as_row(v):
    return jnp.transpose(jnp.broadcast_to(v, (v.shape[0], LANES)))[0:1, :]


def join(m1, l1, m2, l2):
    m = jnp.maximum(m1, m2)
    return m, l1 * jnp.exp(m1 - m) + l2 * jnp.exp(m2 - m)


def statistics(s, row, col, step, ids, mates, multiplier, own):
    tops, lows, top, pos, low = [], [], None, F32(0.0), F32(0.0)
    starts = range(row.start, row.stop, step)
    for at in starts:
        r = slice(at, at + step)
        v = s[r, col] * multiplier
        pos += jnp.sum(jnp.where(ids[:, col] == mates[r, 0:1], v, F32(0.0)), axis=0, keepdims=True)
        if own and at == 0:
            row_ids = lax.broadcasted_iota(jnp.int32, v.shape, 0)
            col_ids = lax.broadcasted_iota(jnp.int32, v.shape, 1) + col.start
            v = jnp.where(row_ids == col_ids, F32(-1e30), v)
        s[r, col] = v
        m = jnp.max(v, axis=1, keepdims=True)
        tops.append(as_row(m))
        lows.append(as_row(jnp.sum(jnp.exp(v - m), axis=1, keepdims=True)))
        m = jnp.max(v, axis=0, keepdims=True)
        top = m if top is None else jnp.maximum(top, m)
    for at in starts:
        low += jnp.sum(jnp.exp(s[at : at + step, col] - top), axis=0, keepdims=True)
    return jnp.concatenate(tops, 1), jnp.concatenate(lows, 1), top, low, pos


def put_mates(r, mates, at):
    n, width = r.shape[0], r.shape[1] - LANES
    two = r[:, width:].astype(F32)
    mates[at : at + n, :] = jnp.broadcast_to(two[:, 0:1] * F32(64.0) + two[:, 1:2], (n, LANES))


def near_kernel(mult, v, zd, zu, b, bo, cols, s1, s2, known1, known2, a, mates):
    step, n, width = v.shape[0], s1.shape[0], a.shape[1]
    at = 0
    for r in (v, zd, zu):
        a[at : at + step, :] = r[:, :width]
        put_mates(r, mates, at)
        at += step
    s1[...] = dot(a[...], b[...], NT)
    s2[...] = dot(a[...], bo[...], NT)
    side = cols.shape[1] // 2
    for s, known, first in ((s1, known1, 0), (s2, known2, side)):
        ids = cols[:, first : first + n]
        found = statistics(s, slice(0, n), slice(0, n), step, ids, mates, mult[0], first == 0)
        known[...] = jnp.zeros(known.shape, F32)
        for i, line in enumerate(found):
            known[i : i + 1, :] = line


def complete(s, tile, known, a, b, t, ids, mates, multiplier, own):
    n, side = tile.shape[0], s.shape[0]
    step = side - n
    s[0:n, 0:n] = tile[...]
    s[n:, 0:n] = dot(a[n:, :], b[...], NT)
    s[:, n:] = dot(a[...], t[...], NT)
    rm0, rl0, cm0, cl0, pos0 = (known[i : i + 1, :] for i in range(5))
    rm1, rl1, cm1, cl1, pos1 = statistics(
        s, slice(0, n), slice(n, side), step, ids, mates, multiplier, own
    )
    rm2, rl2, cm2, cl2, pos2 = statistics(
        s, slice(n, side), slice(0, side), step, ids, mates, multiplier, own
    )
    rm, rl = join(rm0, rl0, rm1, rl1)
    cat = lambda x, y: jnp.concatenate([x, y], 1)
    cm, cl = join(cat(cm0, cm1), cat(cl0, cl1), cm2, cl2)
    return cat(rm, rm2), cat(rl, rl2), cm, cl, cat(pos0, pos1) + pos2


def early_kernel(mult, v, zd, zu, za, zb, b, t, tile, known, cols, a, last, mates, s, rstat, cstat):
    width, w = a.shape[1], last.shape[1]
    at = 0
    for r in (v, zd, zu, za, zb):
        n = r.shape[0]
        a[at : at + n, :] = r[:, :width]
        last[at : at + n, :] = r[:, width - w : width]
        put_mates(r, mates, at)
        at += n
    found = complete(s, tile, known, a, b, t, cols[:, : s.shape[1]], mates, mult[0], True)
    rstat[...] = jnp.zeros(rstat.shape, F32)
    cstat[...] = jnp.zeros(cstat.shape, F32)
    for i, dst in enumerate((rstat, rstat, cstat, cstat, cstat)):
        j = i if i < 2 else i - 2
        dst[j : j + 1, :] = found[i]


def column(row, n):
    return jnp.transpose(jnp.broadcast_to(row, (LANES, n)))[:, :1]


def tail_kernel(mult, a, b, t, tile, known, mates, cols, rs, cs, s, rstat, cstat):
    side = s.shape[1]
    rm, rl, cm, cl, pos = complete(
        s, tile, known, a, b, t, cols[:, side:], mates, mult[0], False
    )
    positive = jnp.sum(cs[2:3, :] + pos, axis=1, keepdims=True)
    rstat[...] = jnp.broadcast_to(positive, rstat.shape)
    rstat[0:1, :], rstat[1:2, :] = join(rs[0:1, :], rs[1:2, :], rm, rl)
    cstat[:, 0:side] = cs[...]
    cstat[:, side:] = jnp.zeros(cs.shape, F32)
    cstat[0:1, side:] = cm
    cstat[1:2, side:] = cl


def merge_kernel(mine, other, r0, r1, r2, r3, out, lse_r):
    wide, rows = out.shape[1], lse_r.shape[1] // 4
    side = wide // 2
    theirs = jnp.concatenate([other[:, side:], other[:, :side]], 1)
    m1, m2 = mine[0:1, :], theirs[0:1, :]
    m = jnp.maximum(m1, m2)
    lse = combine((r0, r1, r2, r3), rows)
    lse_r[...] = jnp.broadcast_to(lse, lse_r.shape)
    positive = r0[2:3, 0:1] + r1[2:3, 0:1] + r2[2:3, 0:1] + r3[2:3, 0:1]
    out[...] = jnp.broadcast_to(jnp.sum(lse, axis=1, keepdims=True) - positive, out.shape)
    out[0:1, :] = m
    out[1:2, :] = mine[1:2, :] * jnp.exp(m1 - m) + theirs[1:2, :] * jnp.exp(m2 - m)


def combine(messages, rows):
    groups = messages[0].shape[1] // (4 * rows)
    tops, lows = [], []
    for step, message in zip(ORDER, messages):
        at = [(g * 4 + ORDER.index((k - step) % 4)) * rows for g in range(groups) for k in ORDER]
        tops.append(jnp.concatenate([message[0:1, p : p + rows] for p in at], 1))
        lows.append(jnp.concatenate([message[1:2, p : p + rows] for p in at], 1))
    top = jnp.maximum(jnp.maximum(tops[0], tops[1]), jnp.maximum(tops[2], tops[3]))
    low = sum(l * jnp.exp(t - top) for t, l in zip(tops, lows))
    return top + jnp.log(low)


def weights_kernel(s1, s2, mates, lse_r, c0, c1, c2, c3, cols, near, far, part):
    tall, side = s1.shape
    lse_c = combine((c0, c1, c2, c3), tall // 4)
    ids = cols[...]

    @pl.loop(0, tall // LANES)
    def _(i):
        r = pl.ds(pl.multiple_of(i * LANES, LANES), LANES)
        mate, lse = mates[r, 0:1], column(lse_r[0:1, r], LANES)
        for s, out, at in ((s1, near, 0), (s2, far, side)):
            v = s[r, :]
            w = jnp.exp(v - lse) + jnp.exp(v - lse_c[:, at : at + side])
            hit = ids[:, at : at + side] == mate
            out[r, :] = (w - jnp.where(hit, F32(2.0), F32(0.0))).astype(BF16)

    part[...] = c0[2:3, 0:LANES] + c1[2:3, 0:LANES] + c2[2:3, 0:LANES] + c3[2:3, 0:LANES]


def pack(dst, at, g):
    n, w = g.shape
    m = jnp.maximum(jnp.max(jnp.abs(g), axis=1, keepdims=True), F32(1e-30))
    k = jnp.ceil(jnp.log(m) * STEPS)
    q = (g * (LEVELS * jnp.exp(k * (-1.0 / STEPS))) + F32(12582912.0)) - F32(12582912.0)
    dst[at : at + n, 0:w] = q.astype(jnp.int32).astype(I16)
    dst[at : at + n, w : w + LANES] = jnp.broadcast_to(k, (n, LANES)).astype(jnp.int32).astype(I16)


def unpack(src, at, n):
    w = src.shape[1] - LANES
    k = src[at : at + n, w : w + LANES].astype(jnp.int32).astype(F32)[:, :1]
    q = src[at : at + n, 0:w].astype(jnp.int32).astype(F32)
    return q * (jnp.exp(k * (1.0 / STEPS)) * (1.0 / LEVELS))


def hand_out(acc, late_fwd, late_bwd, keep1, keep3, own):
    rows = own.shape[0]
    cut = rows // 2
    pack(late_fwd, 0, acc[rows + cut : 2 * rows, :])
    pack(late_bwd, 0, acc[2 * rows : 2 * rows + cut, :])
    keep1[...] = acc[rows : rows + cut, :]
    keep3[...] = acc[2 * rows + cut : 3 * rows, :]
    own[...] = acc[0:rows, :]


def z_terms(near, far, r, w, b, t, bo, to):
    n = b.shape[0]
    return (
        dot(near[r, 0:n], b[:, :w], NN)
        + dot(near[r, n:], t[:, :w], NN)
        + dot(far[r, 0:n], bo[:, :w], NN)
        + dot(far[r, n:], to[:, :w], NN)
    )


def z_first_kernel(near, far, b, t, bo, to, fwd, bwd, acc):
    n, w = acc.shape
    r = slice(near.shape[0] - n, None)
    acc[...] = z_terms(near, far, r, w, b, t, bo, to)
    pack(fwd, 0, acc[0 : n // 2, :])
    pack(bwd, 0, acc[n // 2 :, :])


def z_kernel(near, far, b, t, bo, to, late_fwd, late_bwd, keep1, keep3, own, acc):
    n, w = acc.shape
    acc[...] = z_terms(near, far, slice(0, n), w, b, t, bo, to)
    hand_out(acc, late_fwd, late_bwd, keep1, keep3, own)


def x_first_kernel(near, far, a, o, fwd, bwd, acc):
    n, w = acc.shape[0], a.shape[1] - acc.shape[1]
    r = slice(near.shape[1] - n, None)
    acc[...] = dot(near[:, r], a[:, w:], TN) + dot(far[:, r], o[...], TN)
    pack(fwd, 0, acc[0 : n // 2, :])
    pack(bwd, 0, acc[n // 2 :, :])


def x_kernel(near, far, a, o, late_fwd, late_bwd, keep1, keep3, own, acc):
    n, w = acc.shape[0], a.shape[1] - acc.shape[1]
    acc[...] = dot(near[:, 0:n], a[:, w:], TN) + dot(far[:, 0:n], o[...], TN)
    hand_out(acc, late_fwd, late_bwd, keep1, keep3, own)


def forward_kernel(fwd, bwd, late_fwd, late_bwd, keep1, keep3, to_up, to_down):
    cut = keep1.shape[0]
    pack(to_up, 0, unpack(fwd, 0, cut) + keep1[...])
    pack(to_down, 0, unpack(bwd, 0, cut) + keep3[...])
    to_up[cut:, :] = late_fwd[...]
    to_down[cut:, :] = late_bwd[...]


def finish_kernel(mult, e, oz, uz, dz, ox, ux, dx, grad):
    cut, half = e.shape[0] // 2, oz.shape[1]
    for h in (0, 1):
        r = slice(h * cut, (h + 1) * cut)
        terms = []
        for own, u, d in ((oz, uz, dz), (ox, ux, dx)):
            step, straight = (u, d) if h == 0 else (d, u)
            terms.append(own[r, :] + unpack(step, 0, cut) + unpack(straight, cut, cut))
        g0, g1 = mult[0] * terms[0], mult[0] * terms[1]
        e0, e1 = e[r, :half].astype(F32), e[r, half:].astype(F32)
        square = jnp.sum(e0 * e0, axis=1, keepdims=True) + jnp.sum(e1 * e1, axis=1, keepdims=True)
        factor = lax.rsqrt(square + 1e-06)
        inner = jnp.sum(e0 * g0, axis=1, keepdims=True) + jnp.sum(e1 * g1, axis=1, keepdims=True)
        scale = factor * factor * factor * inner
        grad[r, :half] = (factor * g0 - scale * e0).astype(BF16)
        grad[r, half:] = (factor * g1 - scale * e1).astype(BF16)


def local(embeddings, partner, logit_scale):
    rows, width = embeddings.shape
    cut, side = rows // 2, 4 * rows
    total = rows * 2 * X * Z

    emb = swap(embeddings)
    mate = swap(partner.reshape(1, rows)).reshape(rows, 1)
    digits = jnp.concatenate([mate // 64, mate % 64, jnp.zeros((rows, LANES - 2), jnp.int32)], 1)
    wide = shape(rows, width + LANES, dtype=BF16)
    u, v, cols = call(
        unit_kernel, "unit", (emb, digits.astype(BF16)), (emb, wide, shape(1, 2 * side))
    )

    zu, zd, xu, xd = lax.optimization_barrier((up(v, "z"), down(v, "z"), up(u, "x"), down(u, "x")))
    half_z, half_x = shape(cut, width + LANES, dtype=BF16), shape(cut, width, dtype=BF16)
    xa, xb, za, zb = call(
        halves_kernel, "halves", (xu, xd, zu, zd), (half_x, half_x, half_z, half_z)
    )
    b = stack("stack_b", u, xd, xu)
    bo = other_core(b)
    n = b.shape[0]
    tile1, tile2, known1, known2 = call(
        near_kernel, "near", (logit_scale, v, zd, zu, b, bo, cols),
        (shape(n, n), shape(n, n), shape(8, n), shape(8, n)),
        scratch=[pltpu.VMEM((n, width), BF16), pltpu.VMEM((n, LANES), F32)],
        flops=4 * n * n * width,
    )
    xa, xb, za, zb, tile1, tile2 = lax.optimization_barrier(
        (up(xa, "x"), down(xb, "x"), up(za, "z"), down(zb, "z"), tile1, tile2)
    )
    t = stack("stack_t", xa, xb)
    to = other_core(t)
    along = {"z": width * 9 // 16, "x": width * 7 // 16}
    flops = 2 * side * side * width
    a, last, mates, near, rstat, cstat = call(
        early_kernel, "early", (logit_scale, v, zd, zu, za, zb, b, t, tile1, known1, cols),
        (
            shape(side, width, dtype=BF16), shape(side, along["x"], dtype=BF16),
            shape(side, LANES), shape(side, side), shape(8, side), shape(8, side),
        ),
        flops=flops,
    )
    last_other = other_core(after(last, to))
    far, rstat, cstat = call(
        tail_kernel, "tail", (logit_scale, a, bo, to, tile2, known2, mates, cols, rstat, cstat),
        (shape(side, side), shape(8, side), shape(8, 2 * side)),
        flops=flops,
    )
    cstat_other = other_core(cstat)
    rstats = gather_small(rstat, "z")
    merged, lse_r = call(merge_kernel, "merge", (cstat, cstat_other, *rstats), (cstat, rstat))
    cstats = gather_small(merged, "x")
    near, far, part = call(
        weights_kernel, "weights", (near, far, mates, lse_r, *cstats, cols),
        (shape(side, side, dtype=BF16), shape(side, side, dtype=BF16), shape(1, LANES)),
    )
    far_other = other_core(far)

    def terms(kernels, axis, operands):
        w = along[axis]
        message, kept = shape(cut, w + LANES, dtype=I16), shape(cut, w)
        flops = 4 * side * rows * w
        first = lambda *o: call(
            kernels[0], "first_" + axis, o, (message, message),
            scratch=[pltpu.VMEM((rows, w), F32)], flops=flops,
        )
        rest = lambda *o: call(
            kernels[1], "rest_" + axis, o, (message, message, kept, kept, shape(rows, w)),
            scratch=[pltpu.VMEM((3 * rows, w), F32)], flops=3 * flops, mib=18,
        )
        return first(*operands), rest

    operands_z, operands_x = (near, far, b, t, bo, to), (near, far_other, a, last_other)
    (fz, bz), rest_z = terms((z_first_kernel, z_kernel), "z", operands_z)
    (fx, bx), rest_x = terms((x_first_kernel, x_kernel), "x", operands_x)
    *kept_z, oz = rest_z(after(near, fx), *operands_z[1:])
    *kept_x, ox = rest_x(after(near, oz), *operands_x[1:])
    fz, bz, _ = lax.optimization_barrier((up(fz, "z"), down(bz, "z"), ox))
    fx, bx = up(fx, "x"), down(bx, "x")
    message = {i: shape(rows, w + LANES, dtype=I16) for i, w in along.items()}
    uz, dz = call(forward_kernel, "forward_z", (fz, bz, *kept_z), (message["z"],) * 2)
    uz, dz = up(uz, "z"), down(dz, "z")
    ux, dx = call(forward_kernel, "forward_x", (fx, bx, *kept_x), (message["x"],) * 2)
    ux, dx = up(ux, "x"), down(dx, "x")
    grad, = call(
        finish_kernel, "finish",
        (logit_scale, emb, oz, uz, dz, ox, ux, dx),
        (shape(rows, width, dtype=BF16),),
    )
    part = after(part, grad)
    both = swap(part) + lax.ppermute(part, ("yl", "c"), SWAP_OTHER)
    return swap(grad), (both[0, :1] / total)


def solution(mesh):
    fine = Mesh(
        mesh.devices.reshape(2, X, Z, 2, 2), ("yl", "x", "z", "yh", "c")
    )
    rows = ("yh", "c", "yl", "x", "z")
    return jax.shard_map(
        local,
        mesh=fine,
        in_specs=(P(rows, None), P(rows), P()),
        out_specs=(P(rows, None), P(("yh", "c"))),
        check_vma=False,
    )
```

```python
import functools
import math

import jax
import jax.numpy as jnp
from jax import lax
from jax.experimental import pallas as pl
from jax.experimental.pallas import tpu as pltpu
from jax.sharding import Mesh, PartitionSpec as P

X, Z = 4, 4
ORDER = (0, 1, 3, 2)
LANES = 128
LEVELS = 32000.0
STEPS = 64 / math.log(2.0)
NN = (((1,), (0,)), ((), ()))
NT = (((1,), (1,)), ((), ()))
TN = (((0,), (0,)), ((), ()))
F32, BF16, I16 = jnp.float32, jnp.bfloat16, jnp.int16


def ring(n, step):
    return [(i, (i + step) % n) for i in range(n)]


SWAP = [(0, 0), (1, 2), (2, 1), (3, 3)]
SWAP_OTHER = [(1, 0), (3, 1), (0, 2), (2, 3)]


def swap(v):
    return lax.ppermute(v, ("yl", "c"), SWAP)


def other_core(v):
    return lax.ppermute(v, "c", ring(2, 1))


def up(v, axis):
    return lax.ppermute(v, axis, ring(4, 1))


def down(v, axis):
    return lax.ppermute(v, axis, ring(4, -1))


def after(v, *others):
    return lax.optimization_barrier((v, *others))[0]


def gather_small(v, axis):
    return [v] + [lax.ppermute(v, axis, ring(4, -k)) for k in ORDER[1:]]


def dot(a, b, dims):
    return lax.dot_general(a, b, dims, preferred_element_type=F32)


def call(kernel, name, args, outs, scratch=(), flops=0, mib=14):
    args = [
        pltpu.with_memory_space_constraint(a, pltpu.VMEM) if a.size * a.dtype.itemsize >= 1 << 19 else a
        for a in args
    ]
    vmem = pl.BlockSpec(memory_space=pltpu.VMEM)
    smem = pl.BlockSpec(memory_space=pltpu.SMEM)
    size = sum(a.size * a.dtype.itemsize for a in list(args) + list(outs))
    return pl.pallas_call(
        kernel,
        name=name,
        out_shape=tuple(jax.ShapeDtypeStruct(o.shape, o.dtype) for o in outs),
        in_specs=[smem if a.shape == (1,) else vmem for a in args],
        out_specs=tuple(vmem for _ in outs),
        scratch_shapes=list(scratch),
        cost_estimate=pl.CostEstimate(flops=flops, bytes_accessed=size, transcendentals=0),
        compiler_params=pltpu.CompilerParams(vmem_limit_bytes=mib << 20),
    )(*args)


def shape(*dims, dtype=F32):
    return jax.ShapeDtypeStruct(dims, dtype)


def halves_kernel(xu, xd, zu, zd, xa, xb, za, zb):
    cut = xa.shape[0]
    xa[...] = xu[0:cut, :]
    za[...] = zu[0:cut, :]
    xb[...] = xd[cut:, :]
    zb[...] = zd[cut:, :]


def stack_kernel(*refs):
    at = 0
    for v in refs[:-1]:
        refs[-1][at : at + v.shape[0], :] = v[...]
        at += v.shape[0]


def stack(name, *refs):
    out = shape(sum(r.shape[0] for r in refs), refs[0].shape[1], dtype=BF16)
    return call(stack_kernel, name, refs, (out,))[0]


def unit_kernel(e, digits, u, v, cols):
    rows = e.shape[0]
    c, x, z = lax.axis_index("c"), lax.axis_index("x"), lax.axis_index("z")
    within = lax.broadcasted_iota(jnp.int32, (1, rows), 1)
    for i, cc in enumerate((c, 1 - c)):
        for j, k in enumerate(ORDER):
            first = ((cc * X + lax.rem(x + k, X)) * Z + z) * rows
            at = (4 * i + j) * rows
            cols[:, at : at + rows] = (first + within).astype(F32)
    wide = e[...].astype(F32)
    unit = wide * lax.rsqrt(jnp.sum(wide * wide, axis=1, keepdims=True) + 1e-06)
    u[...] = unit.astype(BF16)
    v[:, : e.shape[1]] = unit.astype(BF16)
    v[:, e.shape[1] :] = digits[...]


def as_row(v):
    return jnp.transpose(jnp.broadcast_to(v, (v.shape[0], LANES)))[0:1, :]


def join(m1, l1, m2, l2):
    m = jnp.maximum(m1, m2)
    return m, l1 * jnp.exp(m1 - m) + l2 * jnp.exp(m2 - m)


def statistics(s, row, col, step, ids, mates, multiplier, own):
    tops, lows, top, pos, low = [], [], None, F32(0.0), F32(0.0)
    starts = range(row.start, row.stop, step)
    for at in starts:
        r = slice(at, at + step)
        v = s[r, col] * multiplier
        pos += jnp.sum(jnp.where(ids[:, col] == mates[r, 0:1], v, F32(0.0)), axis=0, keepdims=True)
        if own and at == 0:
            row_ids = lax.broadcasted_iota(jnp.int32, v.shape, 0)
            col_ids = lax.broadcasted_iota(jnp.int32, v.shape, 1) + col.start
            v = jnp.where(row_ids == col_ids, F32(-1e30), v)
        s[r, col] = v
        m = jnp.max(v, axis=1, keepdims=True)
        tops.append(as_row(m))
        lows.append(as_row(jnp.sum(jnp.exp(v - m), axis=1, keepdims=True)))
        m = jnp.max(v, axis=0, keepdims=True)
        top = m if top is None else jnp.maximum(top, m)
    for at in starts:
        low += jnp.sum(jnp.exp(s[at : at + step, col] - top), axis=0, keepdims=True)
    return jnp.concatenate(tops, 1), jnp.concatenate(lows, 1), top, low, pos


def put_mates(r, mates, at):
    n, width = r.shape[0], r.shape[1] - LANES
    two = r[:, width:].astype(F32)
    mates[at : at + n, :] = jnp.broadcast_to(two[:, 0:1] * F32(64.0) + two[:, 1:2], (n, LANES))


def near_kernel(mult, v, zd, zu, b, bo, cols, s1, s2, known1, known2, a, mates):
    step, n, width = v.shape[0], s1.shape[0], a.shape[1]
    at = 0
    for r in (v, zd, zu):
        a[at : at + step, :] = r[:, :width]
        put_mates(r, mates, at)
        at += step
    s1[...] = dot(a[...], b[...], NT)
    s2[...] = dot(a[...], bo[...], NT)
    side = cols.shape[1] // 2
    for s, known, first in ((s1, known1, 0), (s2, known2, side)):
        ids = cols[:, first : first + n]
        found = statistics(s, slice(0, n), slice(0, n), step, ids, mates, mult[0], first == 0)
        known[...] = jnp.zeros(known.shape, F32)
        for i, line in enumerate(found):
            known[i : i + 1, :] = line


def complete(s, tile, known, a, b, t, ids, mates, multiplier, own):
    n, side = tile.shape[0], s.shape[0]
    step = side - n
    s[0:n, 0:n] = tile[...]
    s[n:, 0:n] = dot(a[n:, :], b[...], NT)
    s[:, n:] = dot(a[...], t[...], NT)
    rm0, rl0, cm0, cl0, pos0 = (known[i : i + 1, :] for i in range(5))
    rm1, rl1, cm1, cl1, pos1 = statistics(
        s, slice(0, n), slice(n, side), step, ids, mates, multiplier, own
    )
    rm2, rl2, cm2, cl2, pos2 = statistics(
        s, slice(n, side), slice(0, side), step, ids, mates, multiplier, own
    )
    rm, rl = join(rm0, rl0, rm1, rl1)
    cat = lambda x, y: jnp.concatenate([x, y], 1)
    cm, cl = join(cat(cm0, cm1), cat(cl0, cl1), cm2, cl2)
    return cat(rm, rm2), cat(rl, rl2), cm, cl, cat(pos0, pos1) + pos2


def early_kernel(mult, v, zd, zu, za, zb, b, t, tile, known, cols, a, last, mates, s, rstat, cstat):
    width, w = a.shape[1], last.shape[1]
    at = 0
    for r in (v, zd, zu, za, zb):
        n = r.shape[0]
        a[at : at + n, :] = r[:, :width]
        last[at : at + n, :] = r[:, width - w : width]
        put_mates(r, mates, at)
        at += n
    found = complete(s, tile, known, a, b, t, cols[:, : s.shape[1]], mates, mult[0], True)
    rstat[...] = jnp.zeros(rstat.shape, F32)
    cstat[...] = jnp.zeros(cstat.shape, F32)
    for i, dst in enumerate((rstat, rstat, cstat, cstat, cstat)):
        j = i if i < 2 else i - 2
        dst[j : j + 1, :] = found[i]


def column(row, n):
    return jnp.transpose(jnp.broadcast_to(row, (LANES, n)))[:, :1]


def tail_kernel(mult, a, b, t, tile, known, mates, cols, rs, cs, s, rstat, cstat):
    side = s.shape[1]
    rm, rl, cm, cl, pos = complete(
        s, tile, known, a, b, t, cols[:, side:], mates, mult[0], False
    )
    positive = jnp.sum(cs[2:3, :] + pos, axis=1, keepdims=True)
    rstat[...] = jnp.broadcast_to(positive, rstat.shape)
    rstat[0:1, :], rstat[1:2, :] = join(rs[0:1, :], rs[1:2, :], rm, rl)
    cstat[:, 0:side] = cs[...]
    cstat[:, side:] = jnp.zeros(cs.shape, F32)
    cstat[0:1, side:] = cm
    cstat[1:2, side:] = cl


def merge_kernel(mine, other, r0, r1, r2, r3, out, lse_r):
    wide, rows = out.shape[1], lse_r.shape[1] // 4
    side = wide // 2
    theirs = jnp.concatenate([other[:, side:], other[:, :side]], 1)
    m1, m2 = mine[0:1, :], theirs[0:1, :]
    m = jnp.maximum(m1, m2)
    lse = combine((r0, r1, r2, r3), rows)
    lse_r[...] = jnp.broadcast_to(lse, lse_r.shape)
    positive = r0[2:3, 0:1] + r1[2:3, 0:1] + r2[2:3, 0:1] + r3[2:3, 0:1]
    out[...] = jnp.broadcast_to(jnp.sum(lse, axis=1, keepdims=True) - positive, out.shape)
    out[0:1, :] = m
    out[1:2, :] = mine[1:2, :] * jnp.exp(m1 - m) + theirs[1:2, :] * jnp.exp(m2 - m)


def combine(messages, rows):
    groups = messages[0].shape[1] // (4 * rows)
    tops, lows = [], []
    for step, message in zip(ORDER, messages):
        at = [(g * 4 + ORDER.index((k - step) % 4)) * rows for g in range(groups) for k in ORDER]
        tops.append(jnp.concatenate([message[0:1, p : p + rows] for p in at], 1))
        lows.append(jnp.concatenate([message[1:2, p : p + rows] for p in at], 1))
    top = jnp.maximum(jnp.maximum(tops[0], tops[1]), jnp.maximum(tops[2], tops[3]))
    low = sum(l * jnp.exp(t - top) for t, l in zip(tops, lows))
    return top + jnp.log(low)


def weights_kernel(s1, s2, mates, lse_r, c0, c1, c2, c3, cols, near, far, part):
    tall, side = s1.shape
    lse_c = combine((c0, c1, c2, c3), tall // 4)
    ids = cols[...]

    @pl.loop(0, tall // LANES)
    def _(i):
        r = pl.ds(pl.multiple_of(i * LANES, LANES), LANES)
        mate, lse = mates[r, 0:1], column(lse_r[0:1, r], LANES)
        for s, out, at in ((s1, near, 0), (s2, far, side)):
            v = s[r, :]
            w = jnp.exp(v - lse) + jnp.exp(v - lse_c[:, at : at + side])
            hit = ids[:, at : at + side] == mate
            out[r, :] = (w - jnp.where(hit, F32(2.0), F32(0.0))).astype(BF16)

    part[...] = c0[2:3, 0:LANES] + c1[2:3, 0:LANES] + c2[2:3, 0:LANES] + c3[2:3, 0:LANES]


def pack(dst, at, g):
    n, w = g.shape
    m = jnp.maximum(jnp.max(jnp.abs(g), axis=1, keepdims=True), F32(1e-30))
    k = jnp.ceil(jnp.log(m) * STEPS)
    q = (g * (LEVELS * jnp.exp(k * (-1.0 / STEPS))) + F32(12582912.0)) - F32(12582912.0)
    dst[at : at + n, 0:w] = q.astype(jnp.int32).astype(I16)
    dst[at : at + n, w : w + LANES] = jnp.broadcast_to(k, (n, LANES)).astype(jnp.int32).astype(I16)


def unpack(src, at, n):
    w = src.shape[1] - LANES
    k = src[at : at + n, w : w + LANES].astype(jnp.int32).astype(F32)[:, :1]
    q = src[at : at + n, 0:w].astype(jnp.int32).astype(F32)
    return q * (jnp.exp(k * (1.0 / STEPS)) * (1.0 / LEVELS))


def hand_out(acc, late_fwd, late_bwd, keep1, keep3, own):
    rows = own.shape[0]
    cut = rows // 2
    pack(late_fwd, 0, acc[rows + cut : 2 * rows, :])
    pack(late_bwd, 0, acc[2 * rows : 2 * rows + cut, :])
    keep1[...] = acc[rows : rows + cut, :]
    keep3[...] = acc[2 * rows + cut : 3 * rows, :]
    own[...] = acc[0:rows, :]


def z_terms(near, far, r, w, b, t, bo, to):
    n = b.shape[0]
    return (
        dot(near[r, 0:n], b[:, :w], NN)
        + dot(near[r, n:], t[:, :w], NN)
        + dot(far[r, 0:n], bo[:, :w], NN)
        + dot(far[r, n:], to[:, :w], NN)
    )


def z_first_kernel(near, far, b, t, bo, to, fwd, bwd, acc):
    n, w = acc.shape
    r = slice(near.shape[0] - n, None)
    acc[...] = z_terms(near, far, r, w, b, t, bo, to)
    pack(fwd, 0, acc[0 : n // 2, :])
    pack(bwd, 0, acc[n // 2 :, :])


def z_kernel(near, far, b, t, bo, to, late_fwd, late_bwd, keep1, keep3, own, acc):
    n, w = acc.shape
    acc[...] = z_terms(near, far, slice(0, n), w, b, t, bo, to)
    hand_out(acc, late_fwd, late_bwd, keep1, keep3, own)


def x_first_kernel(near, far, a, o, fwd, bwd, acc):
    n, w = acc.shape[0], a.shape[1] - acc.shape[1]
    r = slice(near.shape[1] - n, None)
    acc[...] = dot(near[:, r], a[:, w:], TN) + dot(far[:, r], o[...], TN)
    pack(fwd, 0, acc[0 : n // 2, :])
    pack(bwd, 0, acc[n // 2 :, :])


def x_kernel(near, far, a, o, late_fwd, late_bwd, keep1, keep3, own, acc):
    n, w = acc.shape[0], a.shape[1] - acc.shape[1]
    acc[...] = dot(near[:, 0:n], a[:, w:], TN) + dot(far[:, 0:n], o[...], TN)
    hand_out(acc, late_fwd, late_bwd, keep1, keep3, own)


def forward_kernel(fwd, bwd, late_fwd, late_bwd, keep1, keep3, to_up, to_down):
    cut = keep1.shape[0]
    pack(to_up, 0, unpack(fwd, 0, cut) + keep1[...])
    pack(to_down, 0, unpack(bwd, 0, cut) + keep3[...])
    to_up[cut:, :] = late_fwd[...]
    to_down[cut:, :] = late_bwd[...]


def finish_kernel(h, mult, e, oz, uz, dz, ox, ux, dx, grad):
    cut, half = grad.shape[0], oz.shape[1]
    r = slice(h * cut, (h + 1) * cut)
    terms = []
    for own, u, d in ((oz, uz, dz), (ox, ux, dx)):
        step, straight = (u, d) if h == 0 else (d, u)
        terms.append(own[r, :] + unpack(step, 0, cut) + unpack(straight, cut, cut))
    g0, g1 = mult[0] * terms[0], mult[0] * terms[1]
    e0, e1 = e[r, :half].astype(F32), e[r, half:].astype(F32)
    square = jnp.sum(e0 * e0, axis=1, keepdims=True) + jnp.sum(e1 * e1, axis=1, keepdims=True)
    factor = lax.rsqrt(square + 1e-06)
    inner = jnp.sum(e0 * g0, axis=1, keepdims=True) + jnp.sum(e1 * g1, axis=1, keepdims=True)
    scale = factor * factor * factor * inner
    grad[:, :half] = (factor * g0 - scale * e0).astype(BF16)
    grad[:, half:] = (factor * g1 - scale * e1).astype(BF16)


def local(embeddings, partner, logit_scale):
    rows, width = embeddings.shape
    cut, side = rows // 2, 4 * rows
    total = rows * 2 * X * Z

    emb = swap(embeddings)
    mate = swap(partner.reshape(1, rows)).reshape(rows, 1)
    digits = jnp.concatenate([mate // 64, mate % 64, jnp.zeros((rows, LANES - 2), jnp.int32)], 1)
    wide = shape(rows, width + LANES, dtype=BF16)
    u, v, cols = call(
        unit_kernel, "unit", (emb, digits.astype(BF16)), (emb, wide, shape(1, 2 * side))
    )

    zu, zd, xu, xd = lax.optimization_barrier((up(v, "z"), down(v, "z"), up(u, "x"), down(u, "x")))
    half_z, half_x = shape(cut, width + LANES, dtype=BF16), shape(cut, width, dtype=BF16)
    xa, xb, za, zb = call(
        halves_kernel, "halves", (xu, xd, zu, zd), (half_x, half_x, half_z, half_z)
    )
    b = stack("stack_b", u, xd, xu)
    bo = other_core(b)
    n = b.shape[0]
    tile1, tile2, known1, known2 = call(
        near_kernel, "near", (logit_scale, v, zd, zu, b, bo, cols),
        (shape(n, n), shape(n, n), shape(8, n), shape(8, n)),
        scratch=[pltpu.VMEM((n, width), BF16), pltpu.VMEM((n, LANES), F32)],
        flops=4 * n * n * width,
    )
    xa, xb, za, zb, tile1, tile2 = lax.optimization_barrier(
        (up(xa, "x"), down(xb, "x"), up(za, "z"), down(zb, "z"), tile1, tile2)
    )
    t = stack("stack_t", xa, xb)
    to = other_core(t)
    along = {"z": width * 9 // 16, "x": width * 7 // 16}
    flops = 2 * side * side * width
    a, last, mates, near, rstat, cstat = call(
        early_kernel, "early", (logit_scale, v, zd, zu, za, zb, b, t, tile1, known1, cols),
        (
            shape(side, width, dtype=BF16), shape(side, along["x"], dtype=BF16),
            shape(side, LANES), shape(side, side), shape(8, side), shape(8, side),
        ),
        flops=flops,
    )
    last_other = other_core(after(last, to))
    far, rstat, cstat = call(
        tail_kernel, "tail", (logit_scale, a, bo, to, tile2, known2, mates, cols, rstat, cstat),
        (shape(side, side), shape(8, side), shape(8, 2 * side)),
        flops=flops,
    )
    cstat_other = other_core(cstat)
    rstats = gather_small(rstat, "z")
    merged, lse_r = call(merge_kernel, "merge", (cstat, cstat_other, *rstats), (cstat, rstat))
    cstats = gather_small(merged, "x")
    near, far, part = call(
        weights_kernel, "weights", (near, far, mates, lse_r, *cstats, cols),
        (shape(side, side, dtype=BF16), shape(side, side, dtype=BF16), shape(1, LANES)),
    )
    far_other = other_core(far)

    def terms(kernels, axis, operands):
        w = along[axis]
        message, kept = shape(cut, w + LANES, dtype=I16), shape(cut, w)
        flops = 4 * side * rows * w
        first = lambda *o: call(
            kernels[0], "first_" + axis, o, (message, message),
            scratch=[pltpu.VMEM((rows, w), F32)], flops=flops,
        )
        rest = lambda *o: call(
            kernels[1], "rest_" + axis, o, (message, message, kept, kept, shape(rows, w)),
            scratch=[pltpu.VMEM((3 * rows, w), F32)], flops=3 * flops, mib=18,
        )
        return first(*operands), rest

    operands_z, operands_x = (near, far, b, t, bo, to), (near, far_other, a, last_other)
    (fz, bz), rest_z = terms((z_first_kernel, z_kernel), "z", operands_z)
    (fx, bx), rest_x = terms((x_first_kernel, x_kernel), "x", operands_x)
    *kept_z, oz = rest_z(after(near, fx), *operands_z[1:])
    *kept_x, ox = rest_x(after(near, oz), *operands_x[1:])
    fz, bz, _ = lax.optimization_barrier((up(fz, "z"), down(bz, "z"), ox))
    fx, bx = up(fx, "x"), down(bx, "x")
    message = {i: shape(rows, w + LANES, dtype=I16) for i, w in along.items()}
    uz, dz = call(forward_kernel, "forward_z", (fz, bz, *kept_z), (message["z"],) * 2)
    uz, dz = up(uz, "z"), down(dz, "z")
    ux, dx = call(forward_kernel, "forward_x", (fx, bx, *kept_x), (message["x"],) * 2)
    ux, dx = up(ux, "x"), down(dx, "x")
    grads = [
        call(
            functools.partial(finish_kernel, h), "finish",
            (logit_scale, emb, oz, uz, dz, ox, ux, dx), (shape(cut, width, dtype=BF16),),
        )[0]
        for h in (0, 1)
    ]
    part = after(part, *grads)
    both = swap(part) + lax.ppermute(part, ("yl", "c"), SWAP_OTHER)
    return jnp.concatenate([swap(g) for g in grads], 0), (both[0, :1] / total)


def solution(mesh):
    fine = Mesh(
        mesh.devices.reshape(2, X, Z, 2, 2), ("yl", "x", "z", "yh", "c")
    )
    rows = ("yh", "c", "yl", "x", "z")
    return jax.shard_map(
        local,
        mesh=fine,
        in_specs=(P(rows, None), P(rows), P()),
        out_specs=(P(rows, None), P(("yh", "c"))),
        check_vma=False,
    )
```

```python
import functools
import math

import jax
import jax.numpy as jnp
from jax import lax
from jax.experimental import pallas as pl
from jax.experimental.pallas import tpu as pltpu
from jax.sharding import Mesh, PartitionSpec as P

X, Z = 4, 4
ORDER = (0, 1, 3, 2)
LANES = 128
LEVELS = 32000.0
STEPS = 64 / math.log(2.0)
NN = (((1,), (0,)), ((), ()))
NT = (((1,), (1,)), ((), ()))
TN = (((0,), (0,)), ((), ()))
F32, BF16, I16 = jnp.float32, jnp.bfloat16, jnp.int16


def ring(n, step):
    return [(i, (i + step) % n) for i in range(n)]


SWAP = [(0, 0), (1, 2), (2, 1), (3, 3)]
SWAP_OTHER = [(1, 0), (3, 1), (0, 2), (2, 3)]


def swap(v):
    return lax.ppermute(v, ("yl", "c"), SWAP)


def other_core(v):
    return lax.ppermute(v, "c", ring(2, 1))


def up(v, axis):
    return lax.ppermute(v, axis, ring(4, 1))


def down(v, axis):
    return lax.ppermute(v, axis, ring(4, -1))


def after(v, *others):
    return lax.optimization_barrier((v, *others))[0]


def gather_small(v, axis):
    return [v] + [lax.ppermute(v, axis, ring(4, -k)) for k in ORDER[1:]]


def dot(a, b, dims):
    return lax.dot_general(a, b, dims, preferred_element_type=F32)


def call(kernel, name, args, outs, scratch=(), flops=0, mib=14):
    args = [
        pltpu.with_memory_space_constraint(a, pltpu.VMEM) if a.size * a.dtype.itemsize >= 1 << 19 else a
        for a in args
    ]
    vmem = pl.BlockSpec(memory_space=pltpu.VMEM)
    smem = pl.BlockSpec(memory_space=pltpu.SMEM)
    size = sum(a.size * a.dtype.itemsize for a in list(args) + list(outs))
    return pl.pallas_call(
        kernel,
        name=name,
        out_shape=tuple(jax.ShapeDtypeStruct(o.shape, o.dtype) for o in outs),
        in_specs=[smem if a.shape == (1,) else vmem for a in args],
        out_specs=tuple(vmem for _ in outs),
        scratch_shapes=list(scratch),
        cost_estimate=pl.CostEstimate(flops=flops, bytes_accessed=size, transcendentals=0),
        compiler_params=pltpu.CompilerParams(vmem_limit_bytes=mib << 20),
    )(*args)


def shape(*dims, dtype=F32):
    return jax.ShapeDtypeStruct(dims, dtype)


def halves_kernel(xu, xd, zu, zd, xa, xb, za, zb):
    cut = xa.shape[0]
    xa[...] = xu[0:cut, :]
    za[...] = zu[0:cut, :]
    xb[...] = xd[cut:, :]
    zb[...] = zd[cut:, :]


def stack_kernel(*refs):
    at = 0
    for v in refs[:-1]:
        refs[-1][at : at + v.shape[0], :] = v[...]
        at += v.shape[0]


def stack(name, *refs):
    out = shape(sum(r.shape[0] for r in refs), refs[0].shape[1], dtype=BF16)
    return call(stack_kernel, name, refs, (out,))[0]


def unit_kernel(e, digits, u, v, cols):
    rows = e.shape[0]
    c, x, z = lax.axis_index("c"), lax.axis_index("x"), lax.axis_index("z")
    within = lax.broadcasted_iota(jnp.int32, (1, rows), 1)
    for i, cc in enumerate((c, 1 - c)):
        for j, k in enumerate(ORDER):
            first = ((cc * X + lax.rem(x + k, X)) * Z + z) * rows
            at = (4 * i + j) * rows
            cols[:, at : at + rows] = (first + within).astype(F32)
    wide = e[...].astype(F32)
    unit = wide * lax.rsqrt(jnp.sum(wide * wide, axis=1, keepdims=True) + 1e-06)
    u[...] = unit.astype(BF16)
    v[:, : e.shape[1]] = unit.astype(BF16)
    v[:, e.shape[1] :] = digits[...]


def as_row(v):
    return jnp.transpose(jnp.broadcast_to(v, (v.shape[0], LANES)))[0:1, :]


def join(m1, l1, m2, l2):
    m = jnp.maximum(m1, m2)
    return m, l1 * jnp.exp(m1 - m) + l2 * jnp.exp(m2 - m)


def statistics(s, row, col, step, ids, mates, multiplier, own):
    tops, lows, top, pos, low = [], [], None, F32(0.0), F32(0.0)
    starts = range(row.start, row.stop, step)
    for at in starts:
        r = slice(at, at + step)
        v = s[r, col] * multiplier
        pos += jnp.sum(jnp.where(ids[:, col] == mates[r, 0:1], v, F32(0.0)), axis=0, keepdims=True)
        if own and at == 0:
            row_ids = lax.broadcasted_iota(jnp.int32, v.shape, 0)
            col_ids = lax.broadcasted_iota(jnp.int32, v.shape, 1) + col.start
            v = jnp.where(row_ids == col_ids, F32(-1e30), v)
        s[r, col] = v
        m = jnp.max(v, axis=1, keepdims=True)
        tops.append(as_row(m))
        lows.append(as_row(jnp.sum(jnp.exp(v - m), axis=1, keepdims=True)))
        m = jnp.max(v, axis=0, keepdims=True)
        top = m if top is None else jnp.maximum(top, m)
    for at in starts:
        low += jnp.sum(jnp.exp(s[at : at + step, col] - top), axis=0, keepdims=True)
    return jnp.concatenate(tops, 1), jnp.concatenate(lows, 1), top, low, pos


def put_mates(r, mates, at):
    n, width = r.shape[0], r.shape[1] - LANES
    two = r[:, width:].astype(F32)
    mates[at : at + n, :] = jnp.broadcast_to(two[:, 0:1] * F32(64.0) + two[:, 1:2], (n, LANES))


def near_kernel(mult, v, zd, zu, b, bo, cols, s1, s2, known1, known2, a, mates):
    step, n, width = v.shape[0], s1.shape[0], a.shape[1]
    at = 0
    for r in (v, zd, zu):
        a[at : at + step, :] = r[:, :width]
        put_mates(r, mates, at)
        at += step
    s1[...] = dot(a[...], b[...], NT)
    s2[...] = dot(a[...], bo[...], NT)
    side = cols.shape[1] // 2
    for s, known, first in ((s1, known1, 0), (s2, known2, side)):
        ids = cols[:, first : first + n]
        found = statistics(s, slice(0, n), slice(0, n), step, ids, mates, mult[0], first == 0)
        known[...] = jnp.zeros(known.shape, F32)
        for i, line in enumerate(found):
            known[i : i + 1, :] = line


def complete(s, tile, known, a, b, t, ids, mates, multiplier, own):
    n, side = tile.shape[0], s.shape[0]
    step = side - n
    s[0:n, 0:n] = tile[...]
    s[n:, 0:n] = dot(a[n:, :], b[...], NT)
    s[:, n:] = dot(a[...], t[...], NT)
    rm0, rl0, cm0, cl0, pos0 = (known[i : i + 1, :] for i in range(5))
    rm1, rl1, cm1, cl1, pos1 = statistics(
        s, slice(0, n), slice(n, side), step, ids, mates, multiplier, own
    )
    rm2, rl2, cm2, cl2, pos2 = statistics(
        s, slice(n, side), slice(0, side), step, ids, mates, multiplier, own
    )
    rm, rl = join(rm0, rl0, rm1, rl1)
    cat = lambda x, y: jnp.concatenate([x, y], 1)
    cm, cl = join(cat(cm0, cm1), cat(cl0, cl1), cm2, cl2)
    return cat(rm, rm2), cat(rl, rl2), cm, cl, cat(pos0, pos1) + pos2


def early_kernel(mult, v, zd, zu, za, zb, b, t, tile, known, cols, a, last, mates, s, rstat, cstat):
    width, w = a.shape[1], last.shape[1]
    at = 0
    for r in (v, zd, zu, za, zb):
        n = r.shape[0]
        a[at : at + n, :] = r[:, :width]
        last[at : at + n, :] = r[:, width - w : width]
        put_mates(r, mates, at)
        at += n
    found = complete(s, tile, known, a, b, t, cols[:, : s.shape[1]], mates, mult[0], True)
    rstat[...] = jnp.zeros(rstat.shape, F32)
    cstat[...] = jnp.zeros(cstat.shape, F32)
    for i, dst in enumerate((rstat, rstat, cstat, cstat, cstat)):
        j = i if i < 2 else i - 2
        dst[j : j + 1, :] = found[i]


def column(row, n):
    return jnp.transpose(jnp.broadcast_to(row, (LANES, n)))[:, :1]


def tail_kernel(mult, a, b, t, tile, known, mates, cols, rs, cs, s, rstat, cstat):
    side = s.shape[1]
    rm, rl, cm, cl, pos = complete(
        s, tile, known, a, b, t, cols[:, side:], mates, mult[0], False
    )
    positive = jnp.sum(cs[2:3, :] + pos, axis=1, keepdims=True)
    rstat[...] = jnp.broadcast_to(positive, rstat.shape)
    rstat[0:1, :], rstat[1:2, :] = join(rs[0:1, :], rs[1:2, :], rm, rl)
    cstat[:, 0:side] = cs[...]
    cstat[:, side:] = jnp.zeros(cs.shape, F32)
    cstat[0:1, side:] = cm
    cstat[1:2, side:] = cl


def merge_kernel(mine, other, r0, r1, r2, r3, out, lse_r):
    wide, rows = out.shape[1], lse_r.shape[1] // 4
    side = wide // 2
    theirs = jnp.concatenate([other[:, side:], other[:, :side]], 1)
    m1, m2 = mine[0:1, :], theirs[0:1, :]
    m = jnp.maximum(m1, m2)
    lse = combine((r0, r1, r2, r3), rows)
    lse_r[...] = jnp.broadcast_to(lse, lse_r.shape)
    positive = r0[2:3, 0:1] + r1[2:3, 0:1] + r2[2:3, 0:1] + r3[2:3, 0:1]
    out[...] = jnp.broadcast_to(jnp.sum(lse, axis=1, keepdims=True) - positive, out.shape)
    out[0:1, :] = m
    out[1:2, :] = mine[1:2, :] * jnp.exp(m1 - m) + theirs[1:2, :] * jnp.exp(m2 - m)


def combine(messages, rows):
    groups = messages[0].shape[1] // (4 * rows)
    tops, lows = [], []
    for step, message in zip(ORDER, messages):
        at = [(g * 4 + ORDER.index((k - step) % 4)) * rows for g in range(groups) for k in ORDER]
        tops.append(jnp.concatenate([message[0:1, p : p + rows] for p in at], 1))
        lows.append(jnp.concatenate([message[1:2, p : p + rows] for p in at], 1))
    top = jnp.maximum(jnp.maximum(tops[0], tops[1]), jnp.maximum(tops[2], tops[3]))
    low = sum(l * jnp.exp(t - top) for t, l in zip(tops, lows))
    return top + jnp.log(low)


def weights_kernel(s1, s2, mates, lse_r, c0, c1, c2, c3, cols, near, far, part):
    tall, side = s1.shape
    lse_c = combine((c0, c1, c2, c3), tall // 4)
    ids = cols[...]

    @pl.loop(0, tall // LANES)
    def _(i):
        r = pl.ds(pl.multiple_of(i * LANES, LANES), LANES)
        mate, lse = mates[r, 0:1], column(lse_r[0:1, r], LANES)
        for s, out, at in ((s1, near, 0), (s2, far, side)):
            v = s[r, :]
            w = jnp.exp(v - lse) + jnp.exp(v - lse_c[:, at : at + side])
            hit = ids[:, at : at + side] == mate
            out[r, :] = (w - jnp.where(hit, F32(2.0), F32(0.0))).astype(BF16)

    part[...] = c0[2:3, 0:LANES] + c1[2:3, 0:LANES] + c2[2:3, 0:LANES] + c3[2:3, 0:LANES]


def pack(dst, at, g):
    n, w = g.shape
    m = jnp.maximum(jnp.max(jnp.abs(g), axis=1, keepdims=True), F32(1e-30))
    k = jnp.ceil(jnp.log(m) * STEPS)
    q = (g * (LEVELS * jnp.exp(k * (-1.0 / STEPS))) + F32(12582912.0)) - F32(12582912.0)
    dst[at : at + n, 0:w] = q.astype(jnp.int32).astype(I16)
    dst[at : at + n, w : w + LANES] = jnp.broadcast_to(k, (n, LANES)).astype(jnp.int32).astype(I16)


def unpack(src, at, n):
    w = src.shape[1] - LANES
    k = src[at : at + n, w : w + LANES].astype(jnp.int32).astype(F32)[:, :1]
    q = src[at : at + n, 0:w].astype(jnp.int32).astype(F32)
    return q * (jnp.exp(k * (1.0 / STEPS)) * (1.0 / LEVELS))


def hand_out(acc, late_fwd, late_bwd, keep1, keep3, own):
    rows = own.shape[0]
    cut = rows // 2
    pack(late_fwd, 0, acc[rows + cut : 2 * rows, :])
    pack(late_bwd, 0, acc[2 * rows : 2 * rows + cut, :])
    keep1[...] = acc[rows : rows + cut, :]
    keep3[...] = acc[2 * rows + cut : 3 * rows, :]
    own[...] = acc[0:rows, :]


def z_terms(near, far, r, w, b, t, bo, to):
    n = b.shape[0]
    return (
        dot(near[r, 0:n], b[:, :w], NN)
        + dot(near[r, n:], t[:, :w], NN)
        + dot(far[r, 0:n], bo[:, :w], NN)
        + dot(far[r, n:], to[:, :w], NN)
    )


def z_first_kernel(near, far, b, t, bo, to, fwd, bwd, acc):
    n, w = acc.shape
    r = slice(near.shape[0] - n, None)
    acc[...] = z_terms(near, far, r, w, b, t, bo, to)
    pack(fwd, 0, acc[0 : n // 2, :])
    pack(bwd, 0, acc[n // 2 :, :])


def z_kernel(near, far, b, t, bo, to, late_fwd, late_bwd, keep1, keep3, own, acc):
    n, w = acc.shape
    acc[...] = z_terms(near, far, slice(0, n), w, b, t, bo, to)
    hand_out(acc, late_fwd, late_bwd, keep1, keep3, own)


def x_first_kernel(near, far, a, o, fwd, bwd, acc):
    n, w = acc.shape[0], a.shape[1] - acc.shape[1]
    r = slice(near.shape[1] - n, None)
    acc[...] = dot(near[:, r], a[:, w:], TN) + dot(far[:, r], o[...], TN)
    pack(fwd, 0, acc[0 : n // 2, :])
    pack(bwd, 0, acc[n // 2 :, :])


def x_kernel(near, far, a, o, late_fwd, late_bwd, keep1, keep3, own, acc):
    n, w = acc.shape[0], a.shape[1] - acc.shape[1]
    acc[...] = dot(near[:, 0:n], a[:, w:], TN) + dot(far[:, 0:n], o[...], TN)
    hand_out(acc, late_fwd, late_bwd, keep1, keep3, own)


def forward_kernel(fwd, bwd, late_fwd, late_bwd, keep1, keep3, to_up, to_down):
    cut = keep1.shape[0]
    pack(to_up, 0, unpack(fwd, 0, cut) + keep1[...])
    pack(to_down, 0, unpack(bwd, 0, cut) + keep3[...])
    to_up[cut:, :] = late_fwd[...]
    to_down[cut:, :] = late_bwd[...]


def finish_kernel(h, mult, e, oz, uz, dz, ox, ux, dx, grad):
    cut, half = grad.shape[0], oz.shape[1]
    r = slice(h * cut, (h + 1) * cut)
    terms = []
    for own, u, d in ((oz, uz, dz), (ox, ux, dx)):
        step, straight = (u, d) if h == 0 else (d, u)
        terms.append(own[r, :] + unpack(step, 0, cut) + unpack(straight, cut, cut))
    g0, g1 = mult[0] * terms[0], mult[0] * terms[1]
    e0, e1 = e[r, :half].astype(F32), e[r, half:].astype(F32)
    square = jnp.sum(e0 * e0, axis=1, keepdims=True) + jnp.sum(e1 * e1, axis=1, keepdims=True)
    factor = lax.rsqrt(square + 1e-06)
    inner = jnp.sum(e0 * g0, axis=1, keepdims=True) + jnp.sum(e1 * g1, axis=1, keepdims=True)
    scale = factor * factor * factor * inner
    grad[:, :half] = (factor * g0 - scale * e0).astype(BF16)
    grad[:, half:] = (factor * g1 - scale * e1).astype(BF16)


def local(embeddings, partner, logit_scale):
    rows, width = embeddings.shape
    cut, side = rows // 2, 4 * rows
    total = rows * 2 * X * Z

    emb = swap(embeddings)
    mate = swap(partner.reshape(1, rows)).reshape(rows, 1)
    digits = jnp.concatenate([mate // 64, mate % 64, jnp.zeros((rows, LANES - 2), jnp.int32)], 1)
    wide = shape(rows, width + LANES, dtype=BF16)
    u, v, cols = call(
        unit_kernel, "unit", (emb, digits.astype(BF16)), (emb, wide, shape(1, 2 * side))
    )

    zu, zd, xu, xd = lax.optimization_barrier((up(v, "z"), down(v, "z"), up(u, "x"), down(u, "x")))
    half_z, half_x = shape(cut, width + LANES, dtype=BF16), shape(cut, width, dtype=BF16)
    xa, xb, za, zb = call(
        halves_kernel, "halves", (xu, xd, zu, zd), (half_x, half_x, half_z, half_z)
    )
    b = stack("stack_b", u, xd, xu)
    bo = other_core(b)
    n = b.shape[0]
    tile1, tile2, known1, known2 = call(
        near_kernel, "near", (logit_scale, v, zd, zu, b, bo, cols),
        (shape(n, n), shape(n, n), shape(8, n), shape(8, n)),
        scratch=[pltpu.VMEM((n, width), BF16), pltpu.VMEM((n, LANES), F32)],
        flops=4 * n * n * width,
    )
    xa, xb, za, zb, tile1, tile2 = lax.optimization_barrier(
        (up(xa, "x"), down(xb, "x"), up(za, "z"), down(zb, "z"), tile1, tile2)
    )
    t = stack("stack_t", xa, xb)
    to = other_core(t)
    along = {"z": width * 9 // 16, "x": width * 7 // 16}
    flops = 2 * side * side * width
    a, last, mates, near, rstat, cstat = call(
        early_kernel, "early", (logit_scale, v, zd, zu, za, zb, b, t, tile1, known1, cols),
        (
            shape(side, width, dtype=BF16), shape(side, along["x"], dtype=BF16),
            shape(side, LANES), shape(side, side), shape(8, side), shape(8, side),
        ),
        flops=flops,
    )
    far, rstat, cstat = call(
        tail_kernel, "tail", (logit_scale, a, bo, to, tile2, known2, mates, cols, rstat, cstat),
        (shape(side, side), shape(8, side), shape(8, 2 * side)),
        flops=flops,
    )
    last_other = other_core(after(last, cstat))
    cstat_other = other_core(cstat)
    rstats = gather_small(rstat, "z")
    merged, lse_r = call(merge_kernel, "merge", (cstat, cstat_other, *rstats), (cstat, rstat))
    cstats = gather_small(merged, "x")
    near, far, part = call(
        weights_kernel, "weights", (near, far, mates, lse_r, *cstats, cols),
        (shape(side, side, dtype=BF16), shape(side, side, dtype=BF16), shape(1, LANES)),
    )
    far_other = other_core(far)

    def terms(kernels, axis, operands):
        w = along[axis]
        message, kept = shape(cut, w + LANES, dtype=I16), shape(cut, w)
        flops = 4 * side * rows * w
        first = lambda *o: call(
            kernels[0], "first_" + axis, o, (message, message),
            scratch=[pltpu.VMEM((rows, w), F32)], flops=flops,
        )
        rest = lambda *o: call(
            kernels[1], "rest_" + axis, o, (message, message, kept, kept, shape(rows, w)),
            scratch=[pltpu.VMEM((3 * rows, w), F32)], flops=3 * flops, mib=18,
        )
        return first(*operands), rest

    operands_z, operands_x = (near, far, b, t, bo, to), (near, far_other, a, last_other)
    (fz, bz), rest_z = terms((z_first_kernel, z_kernel), "z", operands_z)
    (fx, bx), rest_x = terms((x_first_kernel, x_kernel), "x", operands_x)
    *kept_z, oz = rest_z(after(near, fx), *operands_z[1:])
    *kept_x, ox = rest_x(after(near, oz), *operands_x[1:])
    fz, bz, _ = lax.optimization_barrier((up(fz, "z"), down(bz, "z"), ox))
    fx, bx = up(fx, "x"), down(bx, "x")
    message = {i: shape(rows, w + LANES, dtype=I16) for i, w in along.items()}
    uz, dz = call(forward_kernel, "forward_z", (fz, bz, *kept_z), (message["z"],) * 2)
    uz, dz = up(uz, "z"), down(dz, "z")
    ux, dx = call(forward_kernel, "forward_x", (fx, bx, *kept_x), (message["x"],) * 2)
    ux, dx = up(ux, "x"), down(dx, "x")
    grads = [
        call(
            functools.partial(finish_kernel, h), "finish",
            (logit_scale, emb, oz, uz, dz, ox, ux, dx), (shape(cut, width, dtype=BF16),),
        )[0]
        for h in (0, 1)
    ]
    part = after(part, *grads)
    both = swap(part) + lax.ppermute(part, ("yl", "c"), SWAP_OTHER)
    return jnp.concatenate([swap(g) for g in grads], 0), (both[0, :1] / total)


def solution(mesh):
    fine = Mesh(
        mesh.devices.reshape(2, X, Z, 2, 2), ("yl", "x", "z", "yh", "c")
    )
    rows = ("yh", "c", "yl", "x", "z")
    return jax.shard_map(
        local,
        mesh=fine,
        in_specs=(P(rows, None), P(rows), P()),
        out_specs=(P(rows, None), P(("yh", "c"))),
        check_vma=False,
    )
```

```python
import functools
import math

import jax
import jax.numpy as jnp
from jax import lax
from jax.experimental import pallas as pl
from jax.experimental.pallas import tpu as pltpu
from jax.sharding import Mesh, PartitionSpec as P

X, Z = 4, 4
ORDER = (0, 1, 3, 2)
LANES = 128
LEVELS = 32000.0
STEPS = 64 / math.log(2.0)
NN = (((1,), (0,)), ((), ()))
NT = (((1,), (1,)), ((), ()))
TN = (((0,), (0,)), ((), ()))
F32, BF16, I16 = jnp.float32, jnp.bfloat16, jnp.int16


def ring(n, step):
    return [(i, (i + step) % n) for i in range(n)]


SWAP = [(0, 0), (1, 2), (2, 1), (3, 3)]
SWAP_OTHER = [(1, 0), (3, 1), (0, 2), (2, 3)]


def swap(v):
    return lax.ppermute(v, ("yl", "c"), SWAP)


def other_core(v):
    return lax.ppermute(v, "c", ring(2, 1))


def up(v, axis):
    return lax.ppermute(v, axis, ring(4, 1))


def down(v, axis):
    return lax.ppermute(v, axis, ring(4, -1))


def after(v, *others):
    return lax.optimization_barrier((v, *others))[0]


def gather_small(v, axis):
    return [v] + [lax.ppermute(v, axis, ring(4, -k)) for k in ORDER[1:]]


def dot(a, b, dims):
    return lax.dot_general(a, b, dims, preferred_element_type=F32)


def call(kernel, name, args, outs, scratch=(), flops=0, mib=14):
    args = [
        pltpu.with_memory_space_constraint(a, pltpu.VMEM) if a.size * a.dtype.itemsize >= 1 << 19 else a
        for a in args
    ]
    vmem = pl.BlockSpec(memory_space=pltpu.VMEM)
    smem = pl.BlockSpec(memory_space=pltpu.SMEM)
    size = sum(a.size * a.dtype.itemsize for a in list(args) + list(outs))
    return pl.pallas_call(
        kernel,
        name=name,
        out_shape=tuple(jax.ShapeDtypeStruct(o.shape, o.dtype) for o in outs),
        in_specs=[smem if a.shape == (1,) else vmem for a in args],
        out_specs=tuple(vmem for _ in outs),
        scratch_shapes=list(scratch),
        cost_estimate=pl.CostEstimate(flops=flops, bytes_accessed=size, transcendentals=0),
        compiler_params=pltpu.CompilerParams(vmem_limit_bytes=mib << 20),
    )(*args)


def shape(*dims, dtype=F32):
    return jax.ShapeDtypeStruct(dims, dtype)


def halves_kernel(xu, xd, zu, zd, xa, xb, za, zb):
    cut = xa.shape[0]
    xa[...] = xu[0:cut, :]
    za[...] = zu[0:cut, :]
    xb[...] = xd[cut:, :]
    zb[...] = zd[cut:, :]


def stack_kernel(*refs):
    at = 0
    for v in refs[:-1]:
        refs[-1][at : at + v.shape[0], :] = v[...]
        at += v.shape[0]


def stack(name, *refs):
    out = shape(sum(r.shape[0] for r in refs), refs[0].shape[1], dtype=BF16)
    return call(stack_kernel, name, refs, (out,))[0]


def unit_kernel(e, digits, u, v, cols):
    rows = e.shape[0]
    c, x, z = lax.axis_index("c"), lax.axis_index("x"), lax.axis_index("z")
    within = lax.broadcasted_iota(jnp.int32, (1, rows), 1)
    for i, cc in enumerate((c, 1 - c)):
        for j, k in enumerate(ORDER):
            first = ((cc * X + lax.rem(x + k, X)) * Z + z) * rows
            at = (4 * i + j) * rows
            cols[:, at : at + rows] = (first + within).astype(F32)
    wide = e[...].astype(F32)
    unit = wide * lax.rsqrt(jnp.sum(wide * wide, axis=1, keepdims=True) + 1e-06)
    u[...] = unit.astype(BF16)
    v[:, : e.shape[1]] = unit.astype(BF16)
    v[:, e.shape[1] :] = digits[...]


def as_row(v):
    return jnp.transpose(jnp.broadcast_to(v, (v.shape[0], LANES)))[0:1, :]


def join(m1, l1, m2, l2):
    m = jnp.maximum(m1, m2)
    return m, l1 * jnp.exp(m1 - m) + l2 * jnp.exp(m2 - m)


def statistics(s, row, col, step, ids, mates, multiplier, own):
    tops, lows, top, pos, low = [], [], None, F32(0.0), F32(0.0)
    starts = range(row.start, row.stop, step)
    for at in starts:
        r = slice(at, at + step)
        v = s[r, col] * multiplier
        pos += jnp.sum(jnp.where(ids[:, col] == mates[r, 0:1], v, F32(0.0)), axis=0, keepdims=True)
        if own and at == 0:
            row_ids = lax.broadcasted_iota(jnp.int32, v.shape, 0)
            col_ids = lax.broadcasted_iota(jnp.int32, v.shape, 1) + col.start
            v = jnp.where(row_ids == col_ids, F32(-1e30), v)
        s[r, col] = v
        m = jnp.max(v, axis=1, keepdims=True)
        tops.append(as_row(m))
        lows.append(as_row(jnp.sum(jnp.exp(v - m), axis=1, keepdims=True)))
        m = jnp.max(v, axis=0, keepdims=True)
        top = m if top is None else jnp.maximum(top, m)
    for at in starts:
        low += jnp.sum(jnp.exp(s[at : at + step, col] - top), axis=0, keepdims=True)
    return jnp.concatenate(tops, 1), jnp.concatenate(lows, 1), top, low, pos


def put_mates(r, mates, at):
    n, width = r.shape[0], r.shape[1] - LANES
    two = r[:, width:].astype(F32)
    mates[at : at + n, :] = jnp.broadcast_to(two[:, 0:1] * F32(64.0) + two[:, 1:2], (n, LANES))


def near_kernel(mult, v, zd, zu, b, bo, cols, s1, s2, known1, known2, a, mates):
    step, n, width = v.shape[0], s1.shape[0], a.shape[1]
    at = 0
    for r in (v, zd, zu):
        a[at : at + step, :] = r[:, :width]
        put_mates(r, mates, at)
        at += step
    s1[...] = dot(a[...], b[...], NT)
    s2[...] = dot(a[...], bo[...], NT)
    side = cols.shape[1] // 2
    for s, known, first in ((s1, known1, 0), (s2, known2, side)):
        ids = cols[:, first : first + n]
        found = statistics(s, slice(0, n), slice(0, n), step, ids, mates, mult[0], first == 0)
        known[...] = jnp.zeros(known.shape, F32)
        for i, line in enumerate(found):
            known[i : i + 1, :] = line


def complete(s, tile, known, a, b, t, ids, mates, multiplier, own):
    n, side = tile.shape[0], s.shape[0]
    step = side - n
    s[0:n, 0:n] = tile[...]
    s[n:, 0:n] = dot(a[n:, :], b[...], NT)
    s[:, n:] = dot(a[...], t[...], NT)
    rm0, rl0, cm0, cl0, pos0 = (known[i : i + 1, :] for i in range(5))
    rm1, rl1, cm1, cl1, pos1 = statistics(
        s, slice(0, n), slice(n, side), step, ids, mates, multiplier, own
    )
    rm2, rl2, cm2, cl2, pos2 = statistics(
        s, slice(n, side), slice(0, side), step, ids, mates, multiplier, own
    )
    rm, rl = join(rm0, rl0, rm1, rl1)
    cat = lambda x, y: jnp.concatenate([x, y], 1)
    cm, cl = join(cat(cm0, cm1), cat(cl0, cl1), cm2, cl2)
    return cat(rm, rm2), cat(rl, rl2), cm, cl, cat(pos0, pos1) + pos2


def early_kernel(mult, v, zd, zu, za, zb, b, t, tile, known, cols, a, last, mates, s, rstat, cstat):
    width, w = a.shape[1], last.shape[1]
    at = 0
    for r in (v, zd, zu, za, zb):
        n = r.shape[0]
        a[at : at + n, :] = r[:, :width]
        last[at : at + n, :] = r[:, width - w : width]
        put_mates(r, mates, at)
        at += n
    found = complete(s, tile, known, a, b, t, cols[:, : s.shape[1]], mates, mult[0], True)
    rstat[...] = jnp.zeros(rstat.shape, F32)
    cstat[...] = jnp.zeros(cstat.shape, F32)
    for i, dst in enumerate((rstat, rstat, cstat, cstat, cstat)):
        j = i if i < 2 else i - 2
        dst[j : j + 1, :] = found[i]


def column(row, n):
    return jnp.transpose(jnp.broadcast_to(row, (LANES, n)))[:, :1]


def tail_kernel(mult, a, b, t, tile, known, mates, cols, rs, cs, s, rstat, cstat):
    side = s.shape[1]
    rm, rl, cm, cl, pos = complete(
        s, tile, known, a, b, t, cols[:, side:], mates, mult[0], False
    )
    positive = jnp.sum(cs[2:3, :] + pos, axis=1, keepdims=True)
    rstat[...] = jnp.broadcast_to(positive, rstat.shape)
    rstat[0:1, :], rstat[1:2, :] = join(rs[0:1, :], rs[1:2, :], rm, rl)
    cstat[:, 0:side] = cs[...]
    cstat[:, side:] = jnp.zeros(cs.shape, F32)
    cstat[0:1, side:] = cm
    cstat[1:2, side:] = cl


def merge_kernel(mine, other, r0, r1, r2, r3, out, lse_r):
    wide, rows = out.shape[1], lse_r.shape[1] // 4
    side = wide // 2
    theirs = jnp.concatenate([other[:, side:], other[:, :side]], 1)
    m1, m2 = mine[0:1, :], theirs[0:1, :]
    m = jnp.maximum(m1, m2)
    lse = combine((r0, r1, r2, r3), rows)
    lse_r[...] = jnp.broadcast_to(lse, lse_r.shape)
    positive = r0[2:3, 0:1] + r1[2:3, 0:1] + r2[2:3, 0:1] + r3[2:3, 0:1]
    out[...] = jnp.broadcast_to(jnp.sum(lse, axis=1, keepdims=True) - positive, out.shape)
    out[0:1, :] = m
    out[1:2, :] = mine[1:2, :] * jnp.exp(m1 - m) + theirs[1:2, :] * jnp.exp(m2 - m)


def combine(messages, rows):
    groups = messages[0].shape[1] // (4 * rows)
    tops, lows = [], []
    for step, message in zip(ORDER, messages):
        at = [(g * 4 + ORDER.index((k - step) % 4)) * rows for g in range(groups) for k in ORDER]
        tops.append(jnp.concatenate([message[0:1, p : p + rows] for p in at], 1))
        lows.append(jnp.concatenate([message[1:2, p : p + rows] for p in at], 1))
    top = jnp.maximum(jnp.maximum(tops[0], tops[1]), jnp.maximum(tops[2], tops[3]))
    low = sum(l * jnp.exp(t - top) for t, l in zip(tops, lows))
    return top + jnp.log(low)


def weights_kernel(s1, s2, mates, lse_r, c0, c1, c2, c3, cols, near, far, part):
    tall, side = s1.shape
    lse_c = combine((c0, c1, c2, c3), tall // 4)
    ids = cols[...]

    @pl.loop(0, tall // LANES)
    def _(i):
        r = pl.ds(pl.multiple_of(i * LANES, LANES), LANES)
        mate, lse = mates[r, 0:1], column(lse_r[0:1, r], LANES)
        for s, out, at in ((s1, near, 0), (s2, far, side)):
            v = s[r, :]
            w = jnp.exp(v - lse) + jnp.exp(v - lse_c[:, at : at + side])
            hit = ids[:, at : at + side] == mate
            out[r, :] = (w - jnp.where(hit, F32(2.0), F32(0.0))).astype(BF16)

    part[...] = c0[2:3, 0:LANES] + c1[2:3, 0:LANES] + c2[2:3, 0:LANES] + c3[2:3, 0:LANES]


def pack(dst, at, g):
    n, w = g.shape
    m = jnp.maximum(jnp.max(jnp.abs(g), axis=1, keepdims=True), F32(1e-30))
    k = jnp.ceil(jnp.log(m) * STEPS)
    q = (g * (LEVELS * jnp.exp(k * (-1.0 / STEPS))) + F32(12582912.0)) - F32(12582912.0)
    dst[at : at + n, 0:w] = q.astype(jnp.int32).astype(I16)
    dst[at : at + n, w : w + LANES] = jnp.broadcast_to(k, (n, LANES)).astype(jnp.int32).astype(I16)


def unpack(src, at, n):
    w = src.shape[1] - LANES
    k = src[at : at + n, w : w + LANES].astype(jnp.int32).astype(F32)[:, :1]
    q = src[at : at + n, 0:w].astype(jnp.int32).astype(F32)
    return q * (jnp.exp(k * (1.0 / STEPS)) * (1.0 / LEVELS))


def hand_out(acc, late_fwd, late_bwd, keep1, keep3, own):
    rows = own.shape[0]
    cut = rows // 2
    pack(late_fwd, 0, acc[rows + cut : 2 * rows, :])
    pack(late_bwd, 0, acc[2 * rows : 2 * rows + cut, :])
    keep1[...] = acc[rows : rows + cut, :]
    keep3[...] = acc[2 * rows + cut : 3 * rows, :]
    own[...] = acc[0:rows, :]


def z_terms(near, far, r, w, b, t, bo, to):
    n = b.shape[0]
    return (
        dot(near[r, 0:n], b[:, :w], NN)
        + dot(near[r, n:], t[:, :w], NN)
        + dot(far[r, 0:n], bo[:, :w], NN)
        + dot(far[r, n:], to[:, :w], NN)
    )


def z_first_kernel(near, far, b, t, bo, to, fwd, bwd, acc):
    n, w = acc.shape
    r = slice(near.shape[0] - n, None)
    acc[...] = z_terms(near, far, r, w, b, t, bo, to)
    pack(fwd, 0, acc[0 : n // 2, :])
    pack(bwd, 0, acc[n // 2 :, :])


def z_kernel(near, far, b, t, bo, to, late_fwd, late_bwd, keep1, keep3, own, acc):
    n, w = acc.shape
    acc[...] = z_terms(near, far, slice(0, n), w, b, t, bo, to)
    hand_out(acc, late_fwd, late_bwd, keep1, keep3, own)


def x_first_kernel(near, far, a, o, fwd, bwd, acc):
    n, w = acc.shape[0], a.shape[1] - acc.shape[1]
    r = slice(near.shape[1] - n, None)
    acc[...] = dot(near[:, r], a[:, w:], TN) + dot(far[:, r], o[...], TN)
    pack(fwd, 0, acc[0 : n // 2, :])
    pack(bwd, 0, acc[n // 2 :, :])


def x_kernel(near, far, a, o, late_fwd, late_bwd, keep1, keep3, own, acc):
    n, w = acc.shape[0], a.shape[1] - acc.shape[1]
    acc[...] = dot(near[:, 0:n], a[:, w:], TN) + dot(far[:, 0:n], o[...], TN)
    hand_out(acc, late_fwd, late_bwd, keep1, keep3, own)


def forward_kernel(fwd, bwd, late_fwd, late_bwd, keep1, keep3, to_up, to_down):
    cut = keep1.shape[0]
    pack(to_up, 0, unpack(fwd, 0, cut) + keep1[...])
    pack(to_down, 0, unpack(bwd, 0, cut) + keep3[...])
    to_up[cut:, :] = late_fwd[...]
    to_down[cut:, :] = late_bwd[...]


def finish_kernel(h, mult, e, oz, uz, dz, ox, ux, dx, grad):
    cut, half = grad.shape[0], oz.shape[1]
    r = slice(h * cut, (h + 1) * cut)
    terms = []
    for own, u, d in ((oz, uz, dz), (ox, ux, dx)):
        step, straight = (u, d) if h == 0 else (d, u)
        terms.append(own[r, :] + unpack(step, 0, cut) + unpack(straight, cut, cut))
    g0, g1 = mult[0] * terms[0], mult[0] * terms[1]
    e0, e1 = e[r, :half].astype(F32), e[r, half:].astype(F32)
    square = jnp.sum(e0 * e0, axis=1, keepdims=True) + jnp.sum(e1 * e1, axis=1, keepdims=True)
    factor = lax.rsqrt(square + 1e-06)
    inner = jnp.sum(e0 * g0, axis=1, keepdims=True) + jnp.sum(e1 * g1, axis=1, keepdims=True)
    scale = factor * factor * factor * inner
    grad[:, :half] = (factor * g0 - scale * e0).astype(BF16)
    grad[:, half:] = (factor * g1 - scale * e1).astype(BF16)


def local(embeddings, partner, logit_scale):
    rows, width = embeddings.shape
    cut, side = rows // 2, 4 * rows
    total = rows * 2 * X * Z

    emb = swap(embeddings)
    mate = swap(partner.reshape(1, rows)).reshape(rows, 1)
    digits = jnp.concatenate([mate // 64, mate % 64, jnp.zeros((rows, LANES - 2), jnp.int32)], 1)
    wide = shape(rows, width + LANES, dtype=BF16)
    u, v, cols = call(
        unit_kernel, "unit", (emb, digits.astype(BF16)), (emb, wide, shape(1, 2 * side))
    )

    zu, zd, xu, xd = lax.optimization_barrier((up(v, "z"), down(v, "z"), up(u, "x"), down(u, "x")))
    half_z, half_x = shape(cut, width + LANES, dtype=BF16), shape(cut, width, dtype=BF16)
    xa, xb, za, zb = call(
        halves_kernel, "halves", (xu, xd, zu, zd), (half_x, half_x, half_z, half_z)
    )
    b = stack("stack_b", u, xd, xu)
    bo = other_core(b)
    n = b.shape[0]
    tile1, tile2, known1, known2 = call(
        near_kernel, "near", (logit_scale, v, zd, zu, b, bo, cols),
        (shape(n, n), shape(n, n), shape(8, n), shape(8, n)),
        scratch=[pltpu.VMEM((n, width), BF16), pltpu.VMEM((n, LANES), F32)],
        flops=4 * n * n * width,
    )
    xa, xb, za, zb, tile1, tile2 = lax.optimization_barrier(
        (up(xa, "x"), down(xb, "x"), up(za, "z"), down(zb, "z"), tile1, tile2)
    )
    t = stack("stack_t", xa, xb)
    to = other_core(t)
    along = {"z": width * 9 // 16, "x": width * 7 // 16}
    flops = 2 * side * side * width
    a, last, mates, near, rstat, cstat = call(
        early_kernel, "early", (logit_scale, v, zd, zu, za, zb, b, t, tile1, known1, cols),
        (
            shape(side, width, dtype=BF16), shape(side, along["x"], dtype=BF16),
            shape(side, LANES), shape(side, side), shape(8, side), shape(8, side),
        ),
        flops=flops,
    )
    last_other = other_core(after(last, to))
    far, rstat, cstat = call(
        tail_kernel, "tail", (logit_scale, a, bo, to, tile2, known2, mates, cols, rstat, cstat),
        (shape(side, side), shape(8, side), shape(8, 2 * side)),
        flops=flops,
    )
    cstat_other = other_core(cstat)
    rstats = gather_small(rstat, "z")
    merged, lse_r = call(merge_kernel, "merge", (cstat, cstat_other, *rstats), (cstat, rstat))
    cstats = gather_small(merged, "x")
    near, far, part = call(
        weights_kernel, "weights", (near, far, mates, lse_r, *cstats, cols),
        (shape(side, side, dtype=BF16), shape(side, side, dtype=BF16), shape(1, LANES)),
    )
    far_other = other_core(far)

    def terms(kernels, axis, operands):
        w = along[axis]
        message, kept = shape(cut, w + LANES, dtype=I16), shape(cut, w)
        flops = 4 * side * rows * w
        first = lambda *o: call(
            kernels[0], "first_" + axis, o, (message, message),
            scratch=[pltpu.VMEM((rows, w), F32)], flops=flops,
        )
        rest = lambda *o: call(
            kernels[1], "rest_" + axis, o, (message, message, kept, kept, shape(rows, w)),
            scratch=[pltpu.VMEM((3 * rows, w), F32)], flops=3 * flops, mib=18,
        )
        return first(*operands), rest

    operands_z, operands_x = (near, far, b, t, bo, to), (near, far_other, a, last_other)
    (fz, bz), rest_z = terms((z_first_kernel, z_kernel), "z", operands_z)
    (fx, bx), rest_x = terms((x_first_kernel, x_kernel), "x", operands_x)
    *kept_z, oz = rest_z(after(near, fx), *operands_z[1:])
    *kept_x, ox = rest_x(after(near, oz), *operands_x[1:])
    fz, bz, _ = lax.optimization_barrier((up(fz, "z"), down(bz, "z"), ox))
    fx, bx = up(fx, "x"), down(bx, "x")
    message = {i: shape(rows, w + LANES, dtype=I16) for i, w in along.items()}
    uz, dz = call(forward_kernel, "forward_z", (fz, bz, *kept_z), (message["z"],) * 2)
    uz, dz = up(uz, "z"), down(dz, "z")
    ux, dx = call(forward_kernel, "forward_x", (fx, bx, *kept_x), (message["x"],) * 2)
    ux, dx = up(ux, "x"), down(dx, "x")
    grads = [
        call(
            functools.partial(finish_kernel, h), "finish",
            (logit_scale, emb, oz, uz, dz, ox, ux, dx), (shape(cut, width, dtype=BF16),),
        )[0]
        for h in (0, 1)
    ]
    part = after(part, *grads)
    both = swap(part) + lax.ppermute(part, ("yl", "c"), SWAP_OTHER)
    grad = embeddings
    for h, g in enumerate(grads):
        grad = lax.dynamic_update_slice(grad, swap(g), (h * cut, 0))
    return grad, (both[0, :1] / total)


def solution(mesh):
    fine = Mesh(
        mesh.devices.reshape(2, X, Z, 2, 2), ("yl", "x", "z", "yh", "c")
    )
    rows = ("yh", "c", "yl", "x", "z")
    return jax.shard_map(
        local,
        mesh=fine,
        in_specs=(P(rows, None), P(rows), P()),
        out_specs=(P(rows, None), P(("yh", "c"))),
        check_vma=False,
    )
```
